256 devices in a mesh: dp: 16 (over z_hi, y), tensor: 16 (over x, z_lo, core).
Axes of the slice: x: 4, y: 4, z: 8 (z_hi: 4, z_lo: 2; z = z_hi * 2 + z_lo), core: 2. Of those that a mesh axis runs over, the one named last changes fastest.
Arguments:
- attn_heads: bfloat16 [2048, 8192], P('dp', 'tensor'), may hold values from -6 to 6
- residual: bfloat16 [2048, 8192], P('dp', 'tensor'), may hold values from -6 to 6
- low_hidden: bfloat16 [2048, 8192], P('dp', 'tensor'), may hold values from -6 to 6
- mid_hidden: bfloat16 [2048, 8192], P('dp', 'tensor'), may hold values from -6 to 6
- out_weight: bfloat16 [8192, 8192], P('tensor', 'dp'), may hold values from -0.0625 to 0.0625
- join_weight: bfloat16 [3, 8192, 8192], P(None, 'tensor', 'dp'), may hold values from -0.0390625 to 0.0390625
- join_gain: float32 [8192], replicated, may hold values from 0.1 to 1.9
Outputs:
- joined_state: bfloat16 [2048, 8192], P(('dp', 'tensor'))
The draws below stay inside these ranges and needn't reach their ends.
All inputs are finite; a program needn't handle non-finite values.
Results may differ from the reference program's by a relative error of at most 0.0039.
Values may be sent and summed in bfloat16 or wider, within the bound.
A program may use at most 64 MiB of HBM per device.

```python
import jax
import jax.numpy as jnp
from jax import lax

D = 8192
TOKENS = 2048


def steps_of(rng, dims, split, least, high):
    factor_of = 1.0
    for dim, blocks in split:
        heights = jax.random.uniform(jax.random.fold_in(jax.random.fold_in(rng, 6), dim), (blocks,), jnp.float32, least / len(split), high / len(split))
        factor_of = factor_of * jnp.repeat(jnp.exp(heights), dims[dim] // blocks).reshape((-1,) + (1,) * (len(dims) - 1 - dim))
    return factor_of


def normal_values(stream_key, shape, spread, reach, shards=(), held_as=jnp.bfloat16):
    level = steps_of(stream_key, shape, shards, -0.22, 0.18) if shards else 1.0
    entries = jax.random.normal(stream_key, shape, jnp.float32) * spread * level
    return jnp.minimum(jnp.maximum(entries, -reach), reach).astype(held_as)


def setup_inputs(seed: int = 0) -> dict:
    seeds = jax.random.split(jax.random.key(seed), 8)
    attn_heads = normal_values(seeds[0], (TOKENS, D), 1.0, 6.0, ((0, 16), (1, 16)))
    residual = normal_values(seeds[1], (TOKENS, D), 1.0, 6.0, ((0, 16), (1, 16)))
    low_hidden = normal_values(seeds[2], (TOKENS, D), 1.0, 6.0, ((0, 16), (1, 16)))
    mid_hidden = normal_values(seeds[3], (TOKENS, D), 1.0, 6.0, ((0, 16), (1, 16)))
    out_weight = normal_values(seeds[4], (D, D), D ** -0.5, 0.0625, ((0, 16), (1, 16)))
    join_weight = normal_values(seeds[5], (3, D, D), (3 * D) ** -0.5, 0.0390625, ((1, 16), (2, 16)))
    join_gain = jnp.clip(1.0 + 0.18 * jax.random.normal(seeds[6], (D,), jnp.float32), 0.1, 1.9)
    return {"attn_heads": attn_heads, "residual": residual, "low_hidden": low_hidden, "mid_hidden": mid_hidden, "out_weight": out_weight, "join_weight": join_weight, "join_gain": join_gain}


def reference(attn_heads, residual, low_hidden, mid_hidden, out_weight, join_weight, join_gain):
    head_sum = jnp.dot(attn_heads, out_weight, preferred_element_type=jnp.float32)
    top_hidden = (residual.astype(jnp.float32) + head_sum).astype(jnp.bfloat16)
    joined_sum = jnp.dot(low_hidden, join_weight[0], preferred_element_type=jnp.float32)
    joined_sum = joined_sum + jnp.dot(mid_hidden, join_weight[1], preferred_element_type=jnp.float32)
    joined_sum = joined_sum + jnp.dot(top_hidden, join_weight[2], preferred_element_type=jnp.float32)
    inverse_rms = lax.rsqrt(lax.optimization_barrier(jnp.mean(joined_sum * joined_sum, axis=1, keepdims=True)) + 1e-05)
    return (joined_sum * inverse_rms * join_gain.astype(jnp.float32)).astype(jnp.bfloat16)
```

```python
import functools

import jax
import jax.numpy as jnp
from jax import lax
from jax.experimental import pallas as pl
from jax.experimental.pallas import tpu as pltpu
from jax.sharding import PartitionSpec as P

MESH = pl.DeviceIdType.MESH
F32 = jnp.float32
BF16 = jnp.bfloat16
ORDER = (0, 3, 1, 2)
TOP = 3


def div(a, b):
    return lax.div(a, jnp.int32(b))


def rem(a, b):
    return lax.rem(a, jnp.int32(b))


def kernel(
    attn, resid, low, mid, w_out, w_join, gain, out,
    act, stage, rshard, rpiece, w, snd, rcv, acc, tpiece, jsum, fin,
    x_s, x_r, wl, ws_s, ws_r, wp_s, wp_r, wf_s, wf_r, q_s, q_r,
    z_s, z_r, y_s, y_r, s_s, s_r, p_s, p_r, a_s, a_r,
):
    dp = lax.axis_index("dp")
    tensor = lax.axis_index("tensor")
    zh, y = div(dp, 4), rem(dp, 4)
    pair, u = div(y, 2), rem(y, 2)
    q, c = div(tensor, 2), rem(tensor, 2)
    x, zl = div(q, 2), rem(q, 2)
    other_u, other_c = 1 - u, 1 - c

    def dev(zh_, y_, q_, c_):
        return (zh_ * 4 + y_, q_ * 2 + c_)

    def same(device):
        return jnp.logical_and(device[0] == dp, device[1] == tensor)

    def send(src, dst, ss, rs, device):
        pltpu.make_async_remote_copy(
            src_ref=src, dst_ref=dst, send_sem=ss, recv_sem=rs, device_id=device, device_id_type=MESH
        ).start()

    def wait(ref, sem):
        pltpu.make_async_copy(ref, ref, sem).wait()

    sibling = dev(zh, y, q, other_c)
    partner = dev(zh, 3 - y, q, c)
    across = dev(zh, pair * 2 + other_u, q, c)
    z_up = dev(rem(zh + 1, 4), y, q, c)
    z_down = dev(rem(zh + 3, 4), y, q, c)

    def peer_q(o):
        return rem(x + div(o, 2), 4) * 2 + rem(zl + rem(o, 2), 2)

    def peer(o):
        return dev(zh, y, peer_q(o), c)

    def group(j, du):
        return dev(rem(zh + j, 4), pair * 2 + rem(u + du, 2), q, c)

    def target(j, p):
        yd = y if p == 0 else 3 - y
        return dev(rem(zh + j, 4), pair * 2 + rem(q, 2), zh * 2 + div(yd, 2), c), rem(yd, 2)

    src_p = rem(zl + pair, 2)
    src_j = rem(zh - x + 4, 4)

    def source(fc, jb):
        yd = zl * 2 + fc
        ys = yd + src_p * (3 - 2 * yd)
        return dev(x, ys, 2 * jb + u, c)

    barrier = pltpu.get_barrier_semaphore()

    def greet(device):
        pl.semaphore_signal(barrier, inc=1, device_id=device, device_id_type=MESH)

    greet(sibling)
    greet(partner)
    for o in range(1, 8):
        greet(peer(jnp.int32(o)))
    for o in range(1, 8):
        greet(group(o // 2, o % 2))
    for o in range(8):
        greet(target(o // 2, o % 2)[0])
        greet(source(o // 4, o % 4))

    def split(ref, slot):
        rows = ref[...].astype(F32).reshape(8, 2, 8, 512)
        for half in range(2):
            stage[slot, half] = rows[:, half].reshape(4, 16, 512).astype(BF16)

    split(attn, 0)
    split(resid, 1)
    split(low, 2)
    split(mid, 3)
    act[0, 0, u, c] = stage[0, c]
    rshard[c] = stage[1, c]
    act[1, 0, u, c] = stage[2, c]
    act[2, 0, u, c] = stage[3, c]
    pl.semaphore_wait(barrier, 32)

    def swapped(slot):
        return (act.at[0, 0, u], rshard, act.at[1, 0, u], act.at[2, 0, u])[slot]

    def swap(slot):
        send(stage.at[slot, other_c], swapped(slot).at[c], x_s.at[slot], x_r.at[slot], sibling)

    def weight(k):
        return w_out if k == 0 else w_join.at[k - 1]

    def weight_near(k):
        pltpu.make_async_copy(weight(k), w.at[k, 0, c], wl.at[k]).start()
        send(weight(k), w.at[k, 0, c], ws_s.at[k], ws_r.at[k], sibling)

    def weight_far(k):
        send(weight(k), w.at[k, 1, c], wp_s.at[k], wp_r.at[k], partner)

    def weight_forward(k):
        wait(w.at[k, 1, c], wp_r.at[k])
        send(w.at[k, 1, c], w.at[k, 1, c], wf_s.at[k], wf_r.at[k], sibling)

    def weight_near_ready(k):
        wait(w.at[k, 0, c], wl.at[k])
        wait(w.at[k, 0, other_c], ws_r.at[k])

    def weight_far_ready(k):
        wait(w.at[k, 1, other_c], wf_r.at[k])

    def across_send(a, j):
        send(act.at[a, j, u], act.at[a, j, u], y_s.at[a, j], y_r.at[a, j], across)

    def gather_begin(a):
        send(act.at[a, 0, u], act.at[a, 3, u], z_s.at[a, 0], z_r.at[a, 0], z_up)
        send(act.at[a, 0, u], act.at[a, 1, u], z_s.at[a, 1], z_r.at[a, 1], z_down)
        across_send(a, 0)

    def gather_middle(a):
        wait(act.at[a, 3, u], z_r.at[a, 0])
        send(act.at[a, 3, u, 0], act.at[a, 2, u, 0], z_s.at[a, 2], z_r.at[a, 2], z_up)
        across_send(a, 3)
        wait(act.at[a, 1, u], z_r.at[a, 1])
        send(act.at[a, 1, u, 1], act.at[a, 2, u, 1], z_s.at[a, 3], z_r.at[a, 3], z_down)
        across_send(a, 1)

    def gather_last(a):
        wait(act.at[a, 2, u, 0], z_r.at[a, 2])
        wait(act.at[a, 2, u, 1], z_r.at[a, 3])
        across_send(a, 2)

    def gathered(a, j):
        wait(act.at[a, j, other_u], y_r.at[a, j])

    def product(a, j, p):
        total = None
        for fc in range(2):
            lhs = act[a, j, :, fc].reshape(128, 512)
            term = jnp.dot(lhs, w[a, p, fc], preferred_element_type=F32)
            total = term if total is None else total + term
        return total

    def scatter(s, j, p):
        rcv[s, j, p, 0] = snd[s, j, p, q]

        def body(o, carry):
            send(snd.at[s, j, p, peer_q(o)], rcv.at[s, j, p, o], s_s.at[s, j, p], s_r.at[s, j, p], peer(o))
            return carry

        lax.fori_loop(1, 8, body, 0)

    def head(j, p):
        total = product(0, j, p)
        for jb in range(4):
            for v in range(2):
                start = v * 64 + jb * 16
                snd[0, j, p, 2 * jb + v] = total[start : start + 16].astype(BF16)
        scatter(0, j, p)

    def joined(j, p):
        total = product(TOP, j, p) + acc[j, p]
        for owner in range(8):
            rows = jnp.concatenate([total[8 * owner : 8 * owner + 8], total[64 + 8 * owner : 72 + 8 * owner]], axis=0)
            snd[1, j, p, owner] = rows.astype(BF16)
        scatter(1, j, p)

    def summed(s, j, p):
        wait(rcv.at[s, j, p, pl.ds(1, 7)], s_r.at[s, j, p])
        return jnp.sum(rcv[s, j, p].astype(F32), axis=0)

    def top_piece(j, p):
        total = summed(0, j, p)
        i = j * 2 + p
        wait(rpiece.at[j, p], q_r.at[i])
        tpiece[j, p] = (rpiece[j, p].astype(F32) + total).astype(BF16)
        device, fc = target(j, p)
        jb = div(q, 2)
        me = same(device)
        src, dst, rs = tpiece.at[j, p], act.at[TOP, 0, u, fc, jb], p_r.at[fc, jb]

        @pl.when(me)
        def _():
            pltpu.make_async_copy(src, dst, rs).start()

        @pl.when(jnp.logical_not(me))
        def _():
            send(src, act.at[TOP, 0, rem(q, 2), fc, jb], p_s.at[i], rs, device)

    def residual_piece(fc, jb):
        device = source(fc, jb)
        me = same(device)
        src, dst, rs = rshard.at[fc, jb], rpiece.at[src_j, src_p], q_r.at[src_j * 2 + src_p]

        @pl.when(me)
        def _():
            pltpu.make_async_copy(src, dst, rs).start()

        @pl.when(jnp.logical_not(me))
        def _():
            send(src, dst, q_s.at[fc, jb], rs, device)

    swap(0)
    weight_near(0)
    weight_far(0)
    swap(1)
    swap(2)
    swap(3)
    wait(act.at[0, 0, u, other_c], x_r.at[0])
    gather_begin(0)
    for k in range(1, 4):
        weight_near(k)
    wait(rshard.at[other_c], x_r.at[1])
    for fc in range(2):
        for jb in range(4):
            residual_piece(fc, jb)
    wait(act.at[1, 0, u, other_c], x_r.at[2])
    wait(act.at[2, 0, u, other_c], x_r.at[3])
    weight_near_ready(0)
    gather_middle(0)
    gathered(0, 0)
    head(0, 0)
    gather_last(0)
    gather_begin(1)
    weight_forward(0)
    weight_far(1)
    weight_far(2)
    gathered(0, 3)
    head(3, 0)
    gathered(0, 1)
    head(1, 0)
    weight_far_ready(0)
    head(0, 1)
    head(3, 1)
    head(1, 1)
    gathered(0, 2)
    head(2, 0)
    head(2, 1)
    gather_middle(1)
    gather_last(1)
    gather_begin(2)
    for p in range(2):
        for j in ORDER:
            top_piece(j, p)
    gather_middle(2)
    gather_last(2)
    for fc in range(2):
        for jb in range(4):
            wait(act.at[TOP, 0, u, fc, jb], p_r.at[fc, jb])
    gather_begin(TOP)
    weight_forward(1)
    weight_forward(2)
    weight_far(3)
    gather_middle(TOP)
    gather_last(TOP)
    for a in (1, 2):
        weight_near_ready(a)
        weight_far_ready(a)
        for j in ORDER:
            gathered(a, j)
            for p in range(2):
                acc[j, p] = product(a, j, p) if a == 1 else acc[j, p] + product(a, j, p)
    weight_near_ready(3)
    for j in ORDER:
        gathered(TOP, j)
        joined(j, 0)
    weight_forward(3)
    weight_far_ready(3)
    for j in ORDER:
        joined(j, 1)
    for j in ORDER:
        for p in range(2):
            total = summed(1, j, p)
            jsum[j, 0, p] = total[:8]
            jsum[j, 1, p] = total[8:]
        for du in range(2):
            v = rem(u + du, 2)
            if j == 0 and du == 0:
                fin[zh, u] = jsum[0, u]
            else:
                send(jsum.at[j, v], fin.at[zh, u], a_s.at[j, du], a_r.at[j, du], group(j, du))
    for j in ORDER:
        for du in range(2):
            if j or du:
                wait(fin.at[rem(zh - j + 4, 4), rem(u + du, 2)], a_r.at[j, du])

    squares = jnp.zeros((8, 512), F32)
    for i in range(16):
        block = fin[i // 4, (i // 2) % 2, i % 2]
        squares += block * block
    inverse = lax.rsqrt(jnp.sum(squares, axis=1, keepdims=True) * (1.0 / 8192) + 1e-05)
    for i in range(16):
        zs, us, p = i // 4, (i // 2) % 2, i % 2
        ys = pair * 2 + us if p == 0 else 3 - pair * 2 - us
        columns = pl.ds(pl.multiple_of((zs * 4 + ys) * 512, 512), 512)
        out[:, columns] = fin[zs, us, p] * inverse * gain[:, columns]

    for slot in range(4):
        wait(stage.at[slot, other_c], x_s.at[slot])
        wait(w.at[slot, 0, 0], ws_s.at[slot])
        wait(w.at[slot, 0, 0], wp_s.at[slot])
        wait(w.at[slot, 0, 0], wf_s.at[slot])
        for i in range(4):
            wait(act.at[slot, 0, 0], y_s.at[slot, i])
            wait(act.at[slot, 0, 0] if i < 2 else act.at[slot, 0, 0, 0], z_s.at[slot, i])
    for s in range(2):
        for j in range(4):
            for p in range(2):
                wait(snd.at[s, j, p, pl.ds(1, 7)], s_s.at[s, j, p])
    for i in range(8):
        j, p = i // 2, i % 2

        @pl.when(jnp.logical_not(same(target(j, p)[0])))
        def _():
            wait(tpiece.at[j, p], p_s.at[i])

        fc, jb = i // 4, i % 4

        @pl.when(jnp.logical_not(same(source(fc, jb))))
        def _():
            wait(rshard.at[fc, jb], q_s.at[fc, jb])

        if i:
            wait(jsum.at[0, 0], a_s.at[j, p])


def local(attn_heads, residual, low_hidden, mid_hidden, out_weight, join_weight, join_gain):
    vmem = pl.BlockSpec(memory_space=pltpu.VMEM)
    any_space = pl.BlockSpec(memory_space=pl.ANY)
    dma = pltpu.SemaphoreType.DMA
    rows = pl.pallas_call(
        kernel,
        out_shape=jax.ShapeDtypeStruct((8, 8192), F32),
        in_specs=[vmem] * 4 + [any_space] * 2 + [vmem],
        out_specs=vmem,
        scratch_shapes=[
            pltpu.VMEM((4, 4, 2, 2, 4, 16, 512), BF16),
            pltpu.VMEM((4, 2, 4, 16, 512), BF16),
            pltpu.VMEM((2, 4, 16, 512), BF16),
            pltpu.VMEM((4, 2, 16, 512), BF16),
            pltpu.VMEM((4, 2, 2, 512, 512), BF16),
            pltpu.VMEM((2, 4, 2, 8, 16, 512), BF16),
            pltpu.VMEM((2, 4, 2, 8, 16, 512), BF16),
            pltpu.VMEM((4, 2, 128, 512), F32),
            pltpu.VMEM((4, 2, 16, 512), BF16),
            pltpu.VMEM((4, 2, 2, 8, 512), F32),
            pltpu.VMEM((4, 2, 2, 8, 512), F32),
            dma((4,)), dma((4,)),
            dma((4,)), dma((4,)), dma((4,)), dma((4,)), dma((4,)), dma((4,)), dma((4,)),
            dma((2, 4)), dma((8,)),
            dma((4, 4)), dma((4, 4)), dma((4, 4)), dma((4, 4)),
            dma((2, 4, 2)), dma((2, 4, 2)),
            dma((8,)), dma((2, 4)),
            dma((4, 2)), dma((4, 2)),
        ],
        compiler_params=pltpu.CompilerParams(
            collective_id=0, has_side_effects=True, vmem_limit_bytes=40 * 1024 * 1024
        ),
        cost_estimate=pl.CostEstimate(flops=4294967296, bytes_accessed=3145728, transcendentals=8),
    )(attn_heads, residual, low_hidden, mid_hidden, out_weight, join_weight, join_gain.reshape(1, 8192))
    return rows.astype(BF16)


def solution(mesh):
    return jax.shard_map(
        local,
        mesh=mesh,
        in_specs=(
            P("dp", "tensor"),
            P("dp", "tensor"),
            P("dp", "tensor"),
            P("dp", "tensor"),
            P("tensor", "dp"),
            P(None, "tensor", "dp"),
            P(),
        ),
        out_specs=P(("dp", "tensor"), None),
        check_vma=False,
    )
```

```python
import functools

import jax
import jax.numpy as jnp
from jax import lax
from jax.experimental import pallas as pl
from jax.experimental.pallas import tpu as pltpu
from jax.sharding import PartitionSpec as P

MESH = pl.DeviceIdType.MESH
F32 = jnp.float32
BF16 = jnp.bfloat16
ORDER = (0, 3, 1, 2)
TOP = 3


def div(a, b):
    return lax.div(a, jnp.int32(b))


def rem(a, b):
    return lax.rem(a, jnp.int32(b))


def kernel(
    attn, resid, low, mid, w_out, w_join, gain_in, out,
    inputs, gain, act, stage, rshard, w, snd, rcv, acc, part, half, other, tpiece, tin, jsum, fin,
    in_sem, x_s, x_r, wl, ws_s, ws_r, wp_s, wp_r, wf_s, wf_r,
    z_s, z_r, y_s, y_r, s_s, s_r, h_s, h_r, p_s, p_r, a_s, a_r,
):
    dp = lax.axis_index("dp")
    tensor = lax.axis_index("tensor")
    zh, y = div(dp, 4), rem(dp, 4)
    pair, u = div(y, 2), rem(y, 2)
    q, c = div(tensor, 2), rem(tensor, 2)
    x, zl = div(q, 2), rem(q, 2)
    other_u, other_c = 1 - u, 1 - c

    def dev(zh_, y_, q_, c_):
        return (zh_ * 4 + y_, q_ * 2 + c_)

    def same(device):
        return jnp.logical_and(device[0] == dp, device[1] == tensor)

    def send(src, dst, ss, rs, device):
        pltpu.make_async_remote_copy(
            src_ref=src, dst_ref=dst, send_sem=ss, recv_sem=rs, device_id=device, device_id_type=MESH
        ).start()

    def wait(ref, sem):
        pltpu.make_async_copy(ref, ref, sem).wait()

    sibling = dev(zh, y, q, other_c)
    partner = dev(zh, 3 - y, q, c)
    across = dev(zh, pair * 2 + other_u, q, c)
    z_up = dev(rem(zh + 1, 4), y, q, c)
    z_down = dev(rem(zh + 3, 4), y, q, c)

    def x_of(o):
        return rem(x + o, 4)

    def x_peer(o):
        return dev(zh, y, x_of(o) * 2 + zl, c)

    z_peer = dev(zh, y, x * 2 + 1 - zl, c)

    def group(j, du):
        return dev(rem(zh + j, 4), pair * 2 + rem(u + du, 2), q, c)

    def land(p):
        yd = y if p == 0 else 3 - y
        return div(yd, 2), rem(yd, 2)

    def target(j, p, v):
        return dev(rem(zh + j, 4), pair * 2 + v, zh * 2 + land(p)[0], c)

    def source(fc, xs, zs):
        yd = zl * 2 + fc
        return dev(x, yd + rem(zl + pair, 2) * (3 - 2 * yd), xs * 2 + zs, c)

    loads = [
        pltpu.make_async_copy(ref, inputs.at[i], in_sem.at[i]) for i, ref in enumerate((attn, resid, low, mid))
    ]
    loads.append(pltpu.make_async_copy(gain_in, gain, in_sem.at[4]))
    for load in loads:
        load.start()

    barrier = pltpu.get_barrier_semaphore()

    def greet(device):
        pl.semaphore_signal(barrier, inc=1, device_id=device, device_id_type=MESH)

    greet(sibling)
    greet(partner)
    greet(z_peer)
    for o in range(1, 4):
        greet(x_peer(o))
    for o in range(1, 8):
        greet(group(o // 2, o % 2))
    for i in range(16):
        greet(source(i // 8, i % 8 // 2, i % 2))

    def split(slot):
        loads[slot].wait()
        rows = inputs[slot].astype(F32).reshape(8, 2, 8, 512)
        for half in range(2):
            stage[slot, half] = rows[:, half].reshape(4, 16, 512).astype(BF16)

    def weight(k):
        return w_out if k == 0 else w_join.at[k - 1]

    for k in range(4):
        pltpu.make_async_copy(weight(k), w.at[k, 0, c], wl.at[k]).start()
    for slot in range(4):
        split(slot)
    act[0, 0, u, c] = stage[0, c]
    rshard[c] = stage[1, c]
    act[1, 0, u, c] = stage[2, c]
    act[2, 0, u, c] = stage[3, c]
    pl.semaphore_wait(barrier, 29)

    def swapped(slot):
        return (act.at[0, 0, u], rshard, act.at[1, 0, u], act.at[2, 0, u])[slot]

    def swap(slot):
        send(stage.at[slot, other_c], swapped(slot).at[c], x_s, x_r.at[slot], sibling)

    def weight_near(k):
        send(weight(k), w.at[k, 0, c], ws_s, ws_r.at[k], sibling)

    def weight_far(k):
        send(weight(k), w.at[k, 1, c], wp_s, wp_r.at[k], partner)

    def weight_forward(k):
        wait(w.at[k, 1, c], wp_r.at[k])
        send(w.at[k, 1, c], w.at[k, 1, c], wf_s, wf_r.at[k], sibling)

    def weight_near_ready(k):
        wait(w.at[k, 0, c], wl.at[k])
        wait(w.at[k, 0, other_c], ws_r.at[k])

    def weight_far_ready(k):
        wait(w.at[k, 1, other_c], wf_r.at[k])

    def across_send(a, j, fc):
        piece = act.at[a, j, u, fc]
        send(piece, piece, y_s, y_r.at[a, j], across)

    def z_send(a, slot, fc, to_slot, device):
        send(act.at[a, slot, u, fc], act.at[a, to_slot, u, fc], z_s, z_r.at[a, to_slot - 1, fc], device)

    def z_wait(a, slot, fc):
        wait(act.at[a, slot, u, fc], z_r.at[a, slot - 1, fc])

    def gather_z(a):
        for i in range(2):
            z_send(a, 0, i, 3, z_up)
            z_send(a, 0, 1 - i, 1, z_down)

    def gather_y(a):
        across_send(a, 0, 0)
        across_send(a, 0, 1)

    def gather_first(a):
        z_wait(a, 3, 0)
        z_send(a, 3, 0, 2, z_up)
        across_send(a, 3, 0)
        z_wait(a, 1, 1)
        z_send(a, 1, 1, 2, z_down)
        across_send(a, 1, 1)

    def gather_second(a):
        z_wait(a, 3, 1)
        across_send(a, 3, 1)
        z_wait(a, 1, 0)
        across_send(a, 1, 0)

    def gather_last(a):
        for fc in range(2):
            z_wait(a, 2, fc)
            across_send(a, 2, fc)

    def gathered(a, j):
        wait(act.at[a, j, other_u], y_r.at[a, j])

    def product(a, j, p):
        total = None
        for fc in range(2):
            lhs = act[a, j, :, fc].reshape(128, 512)
            term = jnp.dot(lhs, w[a, p, fc], preferred_element_type=F32)
            total = term if total is None else total + term
        return total

    def scatter(s, j, p):
        for o in range(1, 4):
            send(snd.at[s, j, p, x_of(o)], rcv.at[s, j, p, o - 1], s_s, s_r.at[s, j, p], x_peer(o))

    def head(j, p):
        total = product(0, j, p)
        for v in range(2):
            for jb in range(4):
                start = v * 64 + jb * 16
                part[j, p, jb, v] = total[start : start + 16]
        snd[0, j, p] = part[j, p].astype(BF16)
        scatter(0, j, p)

    def joined(j, p):
        total = product(2, j, p) + acc[j, p] + product(TOP, j, p)
        for owner in range(8):
            rows = jnp.concatenate([total[8 * owner : 8 * owner + 8], total[64 + 8 * owner : 72 + 8 * owner]], axis=0)
            part[j, p, owner // 2, owner % 2] = rows
        snd[1, j, p] = part[j, p].astype(BF16)
        scatter(1, j, p)

    def add_x(s, j, p):
        wait(rcv.at[s, j, p], s_r.at[s, j, p])
        total = part[j, p, x]
        for o in range(3):
            total += rcv[s, j, p, o].astype(F32)
        return total

    def add_head(j, p):
        tpiece[j, p] = add_x(0, j, p).astype(BF16)
        fc = land(p)[1]
        for v in range(2):
            device = target(j, p, v)
            src, dst, rs = tpiece.at[j, p, v], tin.at[fc, x, zl], p_r.at[fc]
            if j:
                send(src, dst, p_s.at[4], rs, device)
            else:
                me = same(device)

                @pl.when(me)
                def _():
                    pltpu.make_async_copy(src, dst, rs).start()

                @pl.when(jnp.logical_not(me))
                def _():
                    send(src, dst, p_s.at[2 * p + v], rs, device)

    def top_rows(fc, jb):
        total = rshard[fc, jb].astype(F32)
        for zs in range(2):
            total += tin[fc, jb, zs].astype(F32)
        act[TOP, 0, u, fc, jb] = total.astype(BF16)

    def add_joined(j, p):
        half[j, p] = add_x(1, j, p)
        send(half.at[j, p, 1 - zl], other.at[j, p], h_s, h_r.at[j, p], z_peer)

    def summed(j, p):
        wait(other.at[j, p], h_r.at[j, p])
        return half[j, p, zl] + other[j, p]

    def deliver(j, p):
        total = summed(j, p)
        jsum[j, 0, p] = total[:8]
        jsum[j, 1, p] = total[8:]
        for du in range(2):
            v = rem(u + du, 2)
            if j == 0 and du == 0:
                fin[zh, u, p] = jsum[0, u, p]
            else:
                send(jsum.at[j, v, p], fin.at[zh, u, p], a_s.at[min(j, 1)], a_r.at[min(j, 1)], group(j, du))

    for slot in range(4):
        swap(slot)
    weight_near(0)
    for k in range(4):
        weight_far(k)
    wait(act.at[0, 0, u, other_c], x_r.at[0])
    gather_z(0)
    gather_y(0)
    wait(rshard.at[other_c], x_r.at[1])
    wait(act.at[1, 0, u, other_c], x_r.at[2])
    wait(act.at[2, 0, u, other_c], x_r.at[3])
    weight_near_ready(0)
    gather_first(0)
    gathered(0, 0)
    head(0, 0)
    gather_second(0)
    gather_z(1)
    weight_near(1)
    weight_forward(0)
    gather_last(0)
    gather_y(1)
    gathered(0, 3)
    head(3, 0)
    weight_far_ready(0)
    head(0, 1)
    head(3, 1)
    gathered(0, 1)
    head(1, 0)
    head(1, 1)
    gather_first(1)
    gather_z(2)
    gathered(0, 2)
    head(2, 0)
    head(2, 1)
    gather_second(1)
    weight_near(2)
    weight_near(3)
    add_head(0, 0)
    add_head(3, 0)
    add_head(0, 1)
    add_head(3, 1)
    gather_last(1)
    gather_y(2)
    add_head(1, 0)
    add_head(1, 1)
    weight_forward(1)
    gather_first(2)
    add_head(2, 0)
    add_head(2, 1)
    gather_second(2)
    for fc in range(2):
        wait(tin.at[fc], p_r.at[fc])
        for jb in range(4):
            top_rows(fc, jb)
    gather_z(TOP)
    gather_last(2)
    gather_y(TOP)
    weight_near_ready(1)
    for j in ORDER:
        gathered(1, j)
    weight_far_ready(1)
    for j in ORDER:
        for p in range(2):
            acc[j, p] = product(1, j, p)
    gather_first(TOP)
    weight_forward(2)
    gather_second(TOP)
    weight_forward(3)
    weight_near_ready(2)
    weight_near_ready(3)
    gathered(2, 0)
    gathered(TOP, 0)
    joined(0, 0)
    gather_last(TOP)
    for j in (3, 1):
        gathered(2, j)
        gathered(TOP, j)
        joined(j, 0)
    weight_far_ready(2)
    gathered(2, 2)
    weight_far_ready(3)
    for j in (0, 3, 1):
        joined(j, 1)
    gathered(TOP, 2)
    joined(2, 0)
    joined(2, 1)
    for p in range(2):
        for j in (0, 3, 1):
            add_joined(j, p)
            if p:
                deliver(j, 0)
    add_joined(2, 0)
    add_joined(2, 1)
    for j in (0, 3, 1):
        deliver(j, 1)
    deliver(2, 0)
    deliver(2, 1)
    wait(stage.at[:, 0], x_s)
    for sem in (ws_s, wp_s, wf_s):
        wait(w.at[:, 0, 0], sem)
    wait(act.at[:, pl.ds(0, 2)], y_s)
    wait(act.at[:, pl.ds(0, 3), 0], z_s)
    wait(snd.at[:, :, :, pl.ds(0, 3)], s_s)
    wait(half.at[:, :, 0], h_s)
    wait(tpiece.at[pl.ds(1, 3)], p_s.at[4])
    for p in range(2):
        for v in range(2):

            @pl.when(jnp.logical_not(same(target(0, p, v))))
            def _():
                wait(tpiece.at[0, p, v], p_s.at[2 * p + v])

    wait(fin.at[0, 0], a_r.at[0])
    wait(fin.at[pl.ds(0, 3)], a_r.at[1])

    squares = jnp.zeros((8, 512), F32)
    for i in range(16):
        block = fin[i // 4, (i // 2) % 2, i % 2]
        squares += block * block
    loads[4].wait()
    inverse = lax.rsqrt(jnp.sum(squares, axis=1, keepdims=True) * (1.0 / 8192) + 1e-05)
    for i in range(16):
        zs, us, p = i // 4, (i // 2) % 2, i % 2
        ys = pair * 2 + us if p == 0 else 3 - pair * 2 - us
        columns = pl.ds(pl.multiple_of((zs * 4 + ys) * 512, 512), 512)
        out[:, columns] = fin[zs, us, p] * inverse * gain[:, columns]

    wait(jsum.at[0, 0], a_s.at[0])
    wait(jsum.at[pl.ds(1, 3)], a_s.at[1])


def local(attn_heads, residual, low_hidden, mid_hidden, out_weight, join_weight, join_gain):
    vmem = pl.BlockSpec(memory_space=pltpu.VMEM)
    hbm = pl.BlockSpec(memory_space=pltpu.HBM)
    dma = pltpu.SemaphoreType.DMA
    rows = pl.pallas_call(
        kernel,
        out_shape=jax.ShapeDtypeStruct((8, 8192), F32),
        in_specs=[hbm] * 7,
        out_specs=vmem,
        scratch_shapes=[
            pltpu.VMEM((4, 128, 512), BF16),
            pltpu.VMEM((1, 8192), F32),
            pltpu.VMEM((4, 4, 2, 2, 4, 16, 512), BF16),
            pltpu.VMEM((4, 2, 4, 16, 512), BF16),
            pltpu.VMEM((2, 4, 16, 512), BF16),
            pltpu.VMEM((4, 2, 2, 512, 512), BF16),
            pltpu.VMEM((2, 4, 2, 4, 2, 16, 512), BF16),
            pltpu.VMEM((2, 4, 2, 3, 2, 16, 512), BF16),
            pltpu.VMEM((4, 2, 128, 512), F32),
            pltpu.VMEM((4, 2, 4, 2, 16, 512), F32),
            pltpu.VMEM((4, 2, 2, 16, 512), F32),
            pltpu.VMEM((4, 2, 16, 512), F32),
            pltpu.VMEM((4, 2, 2, 16, 512), BF16),
            pltpu.VMEM((2, 4, 2, 16, 512), BF16),
            pltpu.VMEM((4, 2, 2, 8, 512), F32),
            pltpu.VMEM((4, 2, 2, 8, 512), F32),
            dma((5,)), dma, dma((4,)),
            dma((4,)), dma, dma((4,)), dma, dma((4,)), dma, dma((4,)),
            dma, dma((4, 3, 2)), dma, dma((4, 4)),
            dma, dma((2, 4, 2)), dma, dma((4, 2)),
            dma((5,)), dma((2,)), dma((2,)), dma((2,)),
        ],
        compiler_params=pltpu.CompilerParams(
            collective_id=0, has_side_effects=True, vmem_limit_bytes=60 * 1024 * 1024
        ),
        cost_estimate=pl.CostEstimate(flops=4294967296, bytes_accessed=3145728, transcendentals=8),
    )(attn_heads, residual, low_hidden, mid_hidden, out_weight, join_weight, join_gain.reshape(1, 8192))
    return rows.astype(BF16)


def solution(mesh):
    return jax.shard_map(
        local,
        mesh=mesh,
        in_specs=(
            P("dp", "tensor"),
            P("dp", "tensor"),
            P("dp", "tensor"),
            P("dp", "tensor"),
            P("tensor", "dp"),
            P(None, "tensor", "dp"),
            P(),
        ),
        out_specs=P(("dp", "tensor"), None),
        check_vma=False,
    )
```

```python
import functools

import jax
import jax.numpy as jnp
from jax import lax
from jax.experimental import pallas as pl
from jax.experimental.pallas import tpu as pltpu
from jax.sharding import PartitionSpec as P

MESH = pl.DeviceIdType.MESH
F32 = jnp.float32
BF16 = jnp.bfloat16
ORDER = (0, 3, 1, 2)
TOP = 3


def div(a, b):
    return lax.div(a, jnp.int32(b))


def rem(a, b):
    return lax.rem(a, jnp.int32(b))


def kernel(
    attn, resid, low, mid, w_out, w_join, gain_in, out,
    inputs, gain, act, stage, rshard, w, snd0, rcv0, snd1, rcv1, acc, part, tpiece, tin, jsum, fin,
    in_sem, x_s, x_r, wl, ws_s, ws_r, wp_s, wp_r, wf_s, wf_r,
    z_s, z_r, y_s, y_r, s_s, s_r, p_s, p_r, a_s, a_r,
):
    dp = lax.axis_index("dp")
    tensor = lax.axis_index("tensor")
    zh, y = div(dp, 4), rem(dp, 4)
    pair, u = div(y, 2), rem(y, 2)
    q, c = div(tensor, 2), rem(tensor, 2)
    x, zl = div(q, 2), rem(q, 2)
    other_u, other_c = 1 - u, 1 - c

    def dev(zh_, y_, q_, c_):
        return (zh_ * 4 + y_, q_ * 2 + c_)

    def same(device):
        return jnp.logical_and(device[0] == dp, device[1] == tensor)

    def send(src, dst, ss, rs, device):
        pltpu.make_async_remote_copy(
            src_ref=src, dst_ref=dst, send_sem=ss, recv_sem=rs, device_id=device, device_id_type=MESH
        ).start()

    def wait(ref, sem):
        pltpu.make_async_copy(ref, ref, sem).wait()

    sibling = dev(zh, y, q, other_c)
    partner = dev(zh, 3 - y, q, c)
    across = dev(zh, pair * 2 + other_u, q, c)
    z_up = dev(rem(zh + 1, 4), y, q, c)
    z_down = dev(rem(zh + 3, 4), y, q, c)

    def x_of(o):
        return rem(x + o, 4)

    def peer(ox, oz):
        return dev(zh, y, x_of(ox) * 2 + rem(zl + oz, 2), c)

    def group(j, du):
        return dev(rem(zh + j, 4), pair * 2 + rem(u + du, 2), q, c)

    def land(p):
        yd = y if p == 0 else 3 - y
        return div(yd, 2), rem(yd, 2)

    def target(j, p, v):
        return dev(rem(zh + j, 4), pair * 2 + v, zh * 2 + land(p)[0], c)

    def source(fc, xs, zs):
        yd = zl * 2 + fc
        return dev(x, yd + rem(zl + pair, 2) * (3 - 2 * yd), xs * 2 + zs, c)

    loads = [
        pltpu.make_async_copy(ref, inputs.at[i], in_sem.at[i]) for i, ref in enumerate((attn, resid, low, mid))
    ]
    loads.append(pltpu.make_async_copy(gain_in, gain, in_sem.at[4]))
    for load in loads:
        load.start()

    barrier = pltpu.get_barrier_semaphore()

    def greet(device):
        pl.semaphore_signal(barrier, inc=1, device_id=device, device_id_type=MESH)

    greet(sibling)
    greet(partner)
    for o in range(1, 8):
        greet(peer(o // 2, o % 2))
    for o in range(1, 8):
        greet(group(o // 2, o % 2))
    for i in range(16):
        greet(source(i // 8, i % 8 // 2, i % 2))

    def split(slot):
        loads[slot].wait()
        rows = inputs[slot].astype(F32).reshape(8, 2, 8, 512)
        for half in range(2):
            stage[slot, half] = rows[:, half].reshape(4, 16, 512).astype(BF16)

    def weight(k):
        return w_out if k == 0 else w_join.at[k - 1]

    for k in range(4):
        pltpu.make_async_copy(weight(k), w.at[k, 0, c], wl.at[k]).start()
    for slot in range(4):
        split(slot)
    act[0, 0, u, c] = stage[0, c]
    rshard[c] = stage[1, c]
    act[1, 0, u, c] = stage[2, c]
    act[2, 0, u, c] = stage[3, c]
    pl.semaphore_wait(barrier, 32)

    def swapped(slot):
        return (act.at[0, 0, u], rshard, act.at[1, 0, u], act.at[2, 0, u])[slot]

    def swap(slot):
        send(stage.at[slot, other_c], swapped(slot).at[c], x_s, x_r.at[slot], sibling)

    def weight_near(k):
        send(weight(k), w.at[k, 0, c], ws_s, ws_r.at[k], sibling)

    def weight_far(k):
        send(weight(k), w.at[k, 1, c], wp_s, wp_r.at[k], partner)

    def weight_forward(k):
        wait(w.at[k, 1, c], wp_r.at[k])
        send(w.at[k, 1, c], w.at[k, 1, c], wf_s, wf_r.at[k], sibling)

    def weight_near_ready(k):
        wait(w.at[k, 0, c], wl.at[k])
        wait(w.at[k, 0, other_c], ws_r.at[k])

    def weight_far_ready(k):
        wait(w.at[k, 1, other_c], wf_r.at[k])

    def across_send(a, j, fc):
        piece = act.at[a, j, u, fc]
        send(piece, piece, y_s, y_r.at[a, j], across)

    def z_send(a, slot, fc, to_slot, device):
        send(act.at[a, slot, u, fc], act.at[a, to_slot, u, fc], z_s, z_r.at[a, to_slot - 1, fc], device)

    def z_wait(a, slot, fc):
        wait(act.at[a, slot, u, fc], z_r.at[a, slot - 1, fc])

    def gather_z(a):
        for i in range(2):
            z_send(a, 0, i, 3, z_up)
            z_send(a, 0, 1 - i, 1, z_down)

    def gather_y(a):
        across_send(a, 0, 0)
        across_send(a, 0, 1)

    def gather_first(a):
        z_wait(a, 3, 0)
        z_send(a, 3, 0, 2, z_up)
        across_send(a, 3, 0)
        z_wait(a, 1, 1)
        z_send(a, 1, 1, 2, z_down)
        across_send(a, 1, 1)

    def gather_second(a):
        z_wait(a, 3, 1)
        across_send(a, 3, 1)
        z_wait(a, 1, 0)
        across_send(a, 1, 0)

    def gather_last(a):
        for fc in range(2):
            z_wait(a, 2, fc)
            across_send(a, 2, fc)

    def gathered(a, j):
        wait(act.at[a, j, other_u], y_r.at[a, j])

    def product(a, j, p):
        total = None
        for fc in range(2):
            lhs = act[a, j, :, fc].reshape(128, 512)
            term = jnp.dot(lhs, w[a, p, fc], preferred_element_type=F32)
            total = term if total is None else total + term
        return total

    def add(own, received):
        total = own
        for o in range(received.shape[0]):
            total += received[o].astype(F32)
        return total

    def head(j, p):
        total = product(0, j, p)
        for v in range(2):
            for jb in range(4):
                start = v * 64 + jb * 16
                part[j, p, jb, v] = total[start : start + 16]
        snd0[j, p] = part[j, p].astype(BF16)
        for o in range(1, 4):
            send(snd0.at[j, p, x_of(o)], rcv0.at[j, p, o - 1], s_s.at[0], s_r.at[0, j, p], peer(o, 0))

    def joined(j, p):
        total = acc[j, p] + product(TOP, j, p)
        for owner in range(8):
            rows = jnp.concatenate([total[8 * owner : 8 * owner + 8], total[64 + 8 * owner : 72 + 8 * owner]], axis=0)
            part[j, p, owner // 2, owner % 2] = rows
            snd1[j, p, owner] = rows.astype(BF16)
        for o in range(1, 8):
            owner = x_of(o // 2) * 2 + rem(zl + o % 2, 2)
            send(snd1.at[j, p, owner], rcv1.at[j, p, o - 1], s_s.at[1], s_r.at[1, j, p], peer(o // 2, o % 2))

    def add_head(j, p):
        wait(rcv0.at[j, p], s_r.at[0, j, p])
        tpiece[j, p] = add(part[j, p, x], rcv0[j, p]).astype(BF16)
        fc = land(p)[1]
        for v in range(2):
            device = target(j, p, v)
            src, dst, rs = tpiece.at[j, p, v], tin.at[fc, x, zl], p_r.at[fc]
            if j:
                send(src, dst, p_s.at[4], rs, device)
            else:
                me = same(device)

                @pl.when(me)
                def _():
                    pltpu.make_async_copy(src, dst, rs).start()

                @pl.when(jnp.logical_not(me))
                def _():
                    send(src, dst, p_s.at[2 * p + v], rs, device)

    def top_rows(fc, jb):
        total = rshard[fc, jb].astype(F32)
        for zs in range(2):
            total += tin[fc, jb, zs].astype(F32)
        act[TOP, 0, u, fc, jb] = total.astype(BF16)

    def deliver(j):
        for p in range(2):
            wait(rcv1.at[j, p], s_r.at[1, j, p])
            total = add(part[j, p, x, zl], rcv1[j, p])
            jsum[j, 0, p] = total[:8]
            jsum[j, 1, p] = total[8:]
        for du in range(2):
            v = rem(u + du, 2)
            if j == 0 and du == 0:
                fin[zh, u] = jsum[0, u]
            else:
                send(jsum.at[j, v], fin.at[zh, u], a_s.at[min(j, 1)], a_r.at[min(j, 1)], group(j, du))

    def add_mid(j):
        gathered(2, j)
        for p in range(2):
            acc[j, p] += product(2, j, p)

    for slot in range(4):
        swap(slot)
    weight_near(0)
    for k in range(4):
        weight_far(k)
    wait(act.at[0, 0, u, other_c], x_r.at[0])
    gather_z(0)
    gather_y(0)
    wait(rshard.at[other_c], x_r.at[1])
    wait(act.at[1, 0, u, other_c], x_r.at[2])
    gather_y(1)
    wait(act.at[2, 0, u, other_c], x_r.at[3])
    weight_near_ready(0)
    gather_first(0)
    gathered(0, 0)
    head(0, 0)
    gather_second(0)
    gather_z(1)
    weight_near(1)
    gather_last(0)
    weight_forward(0)
    gathered(0, 3)
    head(3, 0)
    weight_far_ready(0)
    head(0, 1)
    head(3, 1)
    gathered(0, 1)
    head(1, 0)
    head(1, 1)
    gather_first(1)
    gather_z(2)
    gathered(0, 2)
    head(2, 0)
    head(2, 1)
    gather_second(1)
    weight_near(2)
    weight_near(3)
    add_head(0, 0)
    add_head(3, 0)
    add_head(0, 1)
    add_head(3, 1)
    gather_last(1)
    gather_y(2)
    add_head(1, 0)
    add_head(1, 1)
    weight_forward(1)
    add_head(2, 0)
    add_head(2, 1)
    gather_first(2)
    gather_second(2)
    for fc in range(2):
        wait(tin.at[fc], p_r.at[fc])
        for jb in range(4):
            top_rows(fc, jb)
    gather_z(TOP)
    gather_y(TOP)
    weight_near_ready(1)
    for j in ORDER:
        gathered(1, j)
    weight_far_ready(1)
    for j in ORDER:
        for p in range(2):
            acc[j, p] = product(1, j, p)
    weight_forward(2)
    gather_last(2)
    gather_first(TOP)
    weight_near_ready(2)
    weight_near_ready(3)
    weight_far_ready(2)
    add_mid(0)
    gathered(TOP, 0)
    joined(0, 0)
    gather_second(TOP)
    add_mid(3)
    add_mid(1)
    gather_last(TOP)
    weight_forward(3)
    add_mid(2)
    gathered(TOP, 3)
    joined(3, 0)
    weight_far_ready(3)
    joined(3, 1)
    gathered(TOP, 1)
    joined(1, 0)
    joined(1, 1)
    gathered(TOP, 2)
    joined(2, 0)
    joined(2, 1)
    joined(0, 1)
    for j in (3, 1, 2, 0):
        deliver(j)
    wait(stage.at[:, 0], x_s)
    for sem in (ws_s, wp_s, wf_s):
        wait(w.at[:, 0, 0], sem)
    wait(act.at[:, pl.ds(0, 2)], y_s)
    wait(act.at[:, pl.ds(0, 3), 0], z_s)
    wait(snd0.at[:, :, pl.ds(0, 3)], s_s.at[0])
    wait(snd1.at[:, :, pl.ds(0, 7)], s_s.at[1])
    wait(tpiece.at[pl.ds(1, 3)], p_s.at[4])
    for p in range(2):
        for v in range(2):

            @pl.when(jnp.logical_not(same(target(0, p, v))))
            def _():
                wait(tpiece.at[0, p, v], p_s.at[2 * p + v])

    wait(fin.at[0, 0], a_r.at[0])
    wait(fin.at[pl.ds(0, 3)], a_r.at[1])

    squares = jnp.zeros((8, 512), F32)
    for i in range(16):
        block = fin[i // 4, (i // 2) % 2, i % 2]
        squares += block * block
    loads[4].wait()
    inverse = lax.rsqrt(jnp.sum(squares, axis=1, keepdims=True) * (1.0 / 8192) + 1e-05)
    for i in range(16):
        zs, us, p = i // 4, (i // 2) % 2, i % 2
        ys = pair * 2 + us if p == 0 else 3 - pair * 2 - us
        columns = pl.ds(pl.multiple_of((zs * 4 + ys) * 512, 512), 512)
        out[:, columns] = fin[zs, us, p] * inverse * gain[:, columns]

    wait(jsum.at[0, 0], a_s.at[0])
    wait(jsum.at[pl.ds(1, 3)], a_s.at[1])


def local(attn_heads, residual, low_hidden, mid_hidden, out_weight, join_weight, join_gain):
    vmem = pl.BlockSpec(memory_space=pltpu.VMEM)
    hbm = pl.BlockSpec(memory_space=pltpu.HBM)
    dma = pltpu.SemaphoreType.DMA
    rows = pl.pallas_call(
        kernel,
        out_shape=pltpu.VMEM((8, 8192), F32),
        in_specs=[hbm] * 7,
        out_specs=vmem,
        scratch_shapes=[
            pltpu.VMEM((4, 128, 512), BF16),
            pltpu.VMEM((1, 8192), F32),
            pltpu.VMEM((4, 4, 2, 2, 4, 16, 512), BF16),
            pltpu.VMEM((4, 2, 4, 16, 512), BF16),
            pltpu.VMEM((2, 4, 16, 512), BF16),
            pltpu.VMEM((4, 2, 2, 512, 512), BF16),
            pltpu.VMEM((4, 2, 4, 2, 16, 512), BF16),
            pltpu.VMEM((4, 2, 3, 2, 16, 512), BF16),
            pltpu.VMEM((4, 2, 8, 16, 512), BF16),
            pltpu.VMEM((4, 2, 7, 16, 512), BF16),
            pltpu.VMEM((4, 2, 128, 512), F32),
            pltpu.VMEM((4, 2, 4, 2, 16, 512), F32),
            pltpu.VMEM((4, 2, 2, 16, 512), BF16),
            pltpu.VMEM((2, 4, 2, 16, 512), BF16),
            pltpu.VMEM((4, 2, 2, 8, 512), F32),
            pltpu.VMEM((4, 2, 2, 8, 512), F32),
            dma((5,)), dma, dma((4,)),
            dma((4,)), dma, dma((4,)), dma, dma((4,)), dma, dma((4,)),
            dma, dma((4, 3, 2)), dma, dma((4, 4)),
            dma((2,)), dma((2, 4, 2)),
            dma((5,)), dma((2,)), dma((2,)), dma((2,)),
        ],
        compiler_params=pltpu.CompilerParams(
            collective_id=0, has_side_effects=True, vmem_limit_bytes=60 * 1024 * 1024
        ),
        cost_estimate=pl.CostEstimate(flops=4294967296, bytes_accessed=3145728, transcendentals=8),
    )(attn_heads, residual, low_hidden, mid_hidden, out_weight, join_weight, join_gain.reshape(1, 8192))
    return rows.astype(BF16)


def solution(mesh):
    return jax.shard_map(
        local,
        mesh=mesh,
        in_specs=(
            P("dp", "tensor"),
            P("dp", "tensor"),
            P("dp", "tensor"),
            P("dp", "tensor"),
            P("tensor", "dp"),
            P(None, "tensor", "dp"),
            P(),
        ),
        out_specs=P(("dp", "tensor"), None),
        check_vma=False,
    )
```

```python
import functools

import jax
import jax.numpy as jnp
from jax import lax
from jax.experimental import pallas as pl
from jax.experimental.pallas import tpu as pltpu
from jax.sharding import PartitionSpec as P

MESH = pl.DeviceIdType.MESH
F32 = jnp.float32
BF16 = jnp.bfloat16
ORDER = (0, 3, 1, 2)
TOP = 3


def div(a, b):
    return lax.div(a, jnp.int32(b))


def rem(a, b):
    return lax.rem(a, jnp.int32(b))


def kernel(
    attn, resid, low, mid, w_out, w_join, gain_in, out,
    inputs, gain, act, stage, rshard, w, snd0, rcv0, snd1, rcv1, acc, part, tpiece, tin, rpiece, tdone, jsum, fin,
    in_sem, x_s, x_r, wl, ws_s, ws_r, wp_s, wp_r, wf_s, wf_r,
    z_s, z_r, y_s, y_r, s_s, s_r, p_s, p_r, q_s, q_r, e_s, e_r, a_s, a_r,
):
    dp = lax.axis_index("dp")
    tensor = lax.axis_index("tensor")
    zh, y = div(dp, 4), rem(dp, 4)
    pair, u = div(y, 2), rem(y, 2)
    q, c = div(tensor, 2), rem(tensor, 2)
    x, zl = div(q, 2), rem(q, 2)
    other_u, other_c = 1 - u, 1 - c

    def dev(zh_, y_, q_, c_):
        return (zh_ * 4 + y_, q_ * 2 + c_)

    def same(device):
        return jnp.logical_and(device[0] == dp, device[1] == tensor)

    def send(src, dst, ss, rs, device):
        pltpu.make_async_remote_copy(
            src_ref=src, dst_ref=dst, send_sem=ss, recv_sem=rs, device_id=device, device_id_type=MESH
        ).start()

    def wait(ref, sem):
        pltpu.make_async_copy(ref, ref, sem).wait()

    sibling = dev(zh, y, q, other_c)
    partner = dev(zh, 3 - y, q, c)
    across = dev(zh, pair * 2 + other_u, q, c)
    z_up = dev(rem(zh + 1, 4), y, q, c)
    z_down = dev(rem(zh + 3, 4), y, q, c)

    def x_of(o):
        return rem(x + o, 4)

    def peer(ox, oz):
        return dev(zh, y, x_of(ox) * 2 + rem(zl + oz, 2), c)

    def group(j, du):
        return dev(rem(zh + j, 4), pair * 2 + rem(u + du, 2), q, c)

    def land(p):
        yd = y if p == 0 else 3 - y
        return div(yd, 2), rem(yd, 2)

    def target(j, p, v):
        return dev(rem(zh + j, 4), pair * 2 + v, x * 2 + land(p)[0], c)

    def source(fc, zs, zls):
        yd = zl * 2 + fc
        return dev(zs, yd + rem(zl + pair, 2) * (3 - 2 * yd), x * 2 + zls, c)

    loads = [
        pltpu.make_async_copy(ref, inputs.at[i], in_sem.at[i]) for i, ref in enumerate((attn, resid, low, mid))
    ]
    loads.append(pltpu.make_async_copy(gain_in, gain, in_sem.at[4]))
    for load in loads:
        load.start()

    barrier = pltpu.get_barrier_semaphore()

    def greet(device):
        pl.semaphore_signal(barrier, inc=1, device_id=device, device_id_type=MESH)

    greet(sibling)
    greet(partner)
    for o in range(1, 8):
        greet(peer(o // 2, o % 2))
    for o in range(1, 8):
        greet(group(o // 2, o % 2))
    for i in range(16):
        greet(source(i // 8, i % 8 // 2, i % 2))

    def split(slot):
        loads[slot].wait()
        rows = inputs[slot].astype(F32).reshape(8, 2, 8, 512)
        for half in range(2):
            stage[slot, half] = rows[:, half].reshape(4, 16, 512).astype(BF16)

    def weight(k):
        return w_out if k == 0 else w_join.at[k - 1]

    for k in range(4):
        pltpu.make_async_copy(weight(k), w.at[k, 0, c], wl.at[k]).start()
    for slot in range(4):
        split(slot)
    act[0, 0, u, c] = stage[0, c]
    rshard[c] = stage[1, c]
    act[1, 0, u, c] = stage[2, c]
    act[2, 0, u, c] = stage[3, c]
    pl.semaphore_wait(barrier, 32)

    def swapped(slot):
        return (act.at[0, 0, u], rshard, act.at[1, 0, u], act.at[2, 0, u])[slot]

    def swap(slot):
        send(stage.at[slot, other_c], swapped(slot).at[c], x_s, x_r.at[slot], sibling)

    def weight_near(k):
        send(weight(k), w.at[k, 0, c], ws_s, ws_r.at[k], sibling)

    def weight_far(k):
        send(weight(k), w.at[k, 1, c], wp_s, wp_r.at[k], partner)

    def weight_forward(k):
        wait(w.at[k, 1, c], wp_r.at[k])
        send(w.at[k, 1, c], w.at[k, 1, c], wf_s, wf_r.at[k], sibling)

    def weight_near_ready(k):
        wait(w.at[k, 0, c], wl.at[k])
        wait(w.at[k, 0, other_c], ws_r.at[k])

    def weight_far_ready(k):
        wait(w.at[k, 1, other_c], wf_r.at[k])

    def across_send(a, j, fc):
        piece = act.at[a, j, u, fc]
        send(piece, piece, y_s, y_r.at[a, j], across)

    def z_send(a, slot, fc, to_slot, device):
        send(act.at[a, slot, u, fc], act.at[a, to_slot, u, fc], z_s, z_r.at[a, to_slot - 1, fc], device)

    def z_wait(a, slot, fc):
        wait(act.at[a, slot, u, fc], z_r.at[a, slot - 1, fc])

    def gather_z(a):
        for i in range(2):
            z_send(a, 0, i, 3, z_up)
            z_send(a, 0, 1 - i, 1, z_down)

    def gather_y(a):
        across_send(a, 0, 0)
        across_send(a, 0, 1)

    def gather_first(a):
        z_wait(a, 3, 0)
        z_send(a, 3, 0, 2, z_up)
        across_send(a, 3, 0)
        z_wait(a, 1, 1)
        z_send(a, 1, 1, 2, z_down)
        across_send(a, 1, 1)

    def gather_second(a):
        z_wait(a, 3, 1)
        across_send(a, 3, 1)
        z_wait(a, 1, 0)
        across_send(a, 1, 0)

    def gather_last(a):
        for fc in range(2):
            z_wait(a, 2, fc)
            across_send(a, 2, fc)

    def heads_begin(half):
        z_send(0, 0, half, 3, z_up)
        z_send(0, 0, half, 1, z_down)
        across_send(0, 0, half)

    def heads_first():
        z_wait(0, 3, c)
        z_send(0, 3, c, 2, z_up)
        across_send(0, 3, c)
        z_wait(0, 1, c)
        across_send(0, 1, c)

    def heads_second():
        z_wait(0, 1, other_c)
        z_send(0, 1, other_c, 2, z_down)
        across_send(0, 1, other_c)
        z_wait(0, 3, other_c)
        across_send(0, 3, other_c)

    def gathered(a, j):
        wait(act.at[a, j, other_u], y_r.at[a, j])

    def product(a, j, p):
        total = None
        for fc in range(2):
            lhs = act[a, j, :, fc].reshape(128, 512)
            term = jnp.dot(lhs, w[a, p, fc], preferred_element_type=F32)
            total = term if total is None else total + term
        return total

    def add(own, received):
        total = own
        for o in range(received.shape[0]):
            total += received[o].astype(F32)
        return total

    def head(j, p):
        total = product(0, j, p)
        for v in range(2):
            for jb in range(4):
                start = v * 64 + jb * 16
                part[j, p, jb, v] = total[start : start + 16]
        snd0[j, p] = part[j, p].astype(BF16)
        for o in range(1, 4):
            send(snd0.at[j, p, x_of(o)], rcv0.at[j, p, o - 1], s_s.at[0], s_r.at[0, j, p], peer(o, 0))

    def joined(j, p):
        total = acc[j, p] + product(TOP, j, p)
        for owner in range(8):
            rows = jnp.concatenate([total[8 * owner : 8 * owner + 8], total[64 + 8 * owner : 72 + 8 * owner]], axis=0)
            part[j, p, owner // 2, owner % 2] = rows
            snd1[j, p, owner] = rows.astype(BF16)
        for o in range(1, 8):
            owner = x_of(o // 2) * 2 + rem(zl + o % 2, 2)
            send(snd1.at[j, p, owner], rcv1.at[j, p, o - 1], s_s.at[1], s_r.at[1, j, p], peer(o // 2, o % 2))

    def add_head(j, p):
        wait(rcv0.at[j, p], s_r.at[0, j, p])
        tpiece[j, p] = add(part[j, p, x], rcv0[j, p]).astype(BF16)
        fc = land(p)[1]
        for v in range(2):
            device = target(j, p, v)
            src, dst, rs = tpiece.at[j, p, v], tin.at[zh, fc, zl], p_r.at[zh]
            if j:
                send(src, dst, p_s.at[4], rs, device)
            else:
                me = same(device)

                @pl.when(me)
                def _():
                    pltpu.make_async_copy(src, dst, rs).start()

                @pl.when(jnp.logical_not(me))
                def _():
                    send(src, dst, p_s.at[2 * p + v], rs, device)

    def residual_out():
        for fc in range(2):
            rpiece[x, fc] = rshard[fc, x]
            for o in range(1, 4):
                send(rshard.at[fc, x_of(o)], rpiece.at[x, fc], q_s, q_r, peer(o, 0))

    def top_rows(j):
        zs = rem(zh - j + 4, 4)
        wait(tin.at[zs], p_r.at[zs])
        for fc in range(2):
            total = rpiece[zs, fc].astype(F32)
            for i in range(2):
                total += tin[zs, fc, i].astype(F32)
            tdone[zs, fc] = total.astype(BF16)

        @pl.when(zs == x)
        def _():
            for fc in range(2):
                act[TOP, 0, u, fc, x] = tdone[zs, fc]

        @pl.when(zs != x)
        def _():
            for fc in range(2):
                send(tdone.at[zs, fc], act.at[TOP, 0, u, fc, x], e_s, e_r.at[fc], dev(zh, y, zs * 2 + zl, c))

    def deliver(j):
        for p in range(2):
            wait(rcv1.at[j, p], s_r.at[1, j, p])
            total = add(part[j, p, x, zl], rcv1[j, p])
            jsum[j, 0, p] = total[:8]
            jsum[j, 1, p] = total[8:]
        for du in range(2):
            v = rem(u + du, 2)
            if j == 0 and du == 0:
                fin[zh, u] = jsum[0, u]
            else:
                send(jsum.at[j, v], fin.at[zh, u], a_s.at[min(j, 1)], a_r.at[min(j, 1)], group(j, du))

    def add_mid(j):
        gathered(2, j)
        for p in range(2):
            acc[j, p] += product(2, j, p)

    swap(0)
    heads_begin(c)
    for slot in range(1, 4):
        swap(slot)
    weight_near(0)
    for k in range(4):
        weight_far(k)
    wait(act.at[0, 0, u, other_c], x_r.at[0])
    heads_begin(other_c)
    wait(rshard.at[other_c], x_r.at[1])
    wait(act.at[1, 0, u, other_c], x_r.at[2])
    gather_y(1)
    wait(act.at[2, 0, u, other_c], x_r.at[3])
    weight_near_ready(0)
    heads_first()
    gathered(0, 0)
    head(0, 0)
    heads_second()
    gather_z(1)
    residual_out()
    weight_near(1)
    gather_last(0)
    weight_forward(0)
    gathered(0, 3)
    head(3, 0)
    weight_far_ready(0)
    head(3, 1)
    gathered(0, 1)
    head(1, 0)
    gather_first(1)
    gather_z(2)
    gathered(0, 2)
    head(2, 0)
    head(2, 1)
    head(1, 1)
    head(0, 1)
    gather_second(1)
    weight_near(2)
    weight_near(3)
    add_head(0, 0)
    add_head(3, 0)
    add_head(3, 1)
    gather_last(1)
    gather_y(2)
    add_head(1, 0)
    add_head(2, 0)
    add_head(2, 1)
    weight_forward(1)
    add_head(1, 1)
    add_head(0, 1)
    gather_first(2)
    gather_second(2)
    wait(rpiece.at[pl.ds(0, 3)], q_r)
    for j in ORDER:
        top_rows(j)
    for fc in range(2):
        wait(act.at[TOP, 0, u, fc, pl.ds(0, 3)], e_r.at[fc])
    gather_z(TOP)
    gather_y(TOP)
    weight_near_ready(1)
    for j in ORDER:
        gathered(1, j)
    weight_far_ready(1)
    for j in ORDER:
        for p in range(2):
            acc[j, p] = product(1, j, p)
    weight_forward(2)
    gather_last(2)
    gather_first(TOP)
    weight_near_ready(2)
    weight_near_ready(3)
    weight_far_ready(2)
    add_mid(0)
    gathered(TOP, 0)
    joined(0, 0)
    gather_second(TOP)
    add_mid(3)
    add_mid(1)
    gather_last(TOP)
    weight_forward(3)
    add_mid(2)
    gathered(TOP, 3)
    joined(3, 0)
    weight_far_ready(3)
    joined(3, 1)
    gathered(TOP, 1)
    joined(1, 0)
    gathered(TOP, 2)
    joined(2, 0)
    joined(2, 1)
    joined(1, 1)
    joined(0, 1)
    for j in (3, 2, 1, 0):
        deliver(j)
    wait(stage.at[:, 0], x_s)
    for sem in (ws_s, wp_s, wf_s):
        wait(w.at[:, 0, 0], sem)
    wait(act.at[:, pl.ds(0, 2)], y_s)
    wait(act.at[:, pl.ds(0, 3), 0], z_s)
    wait(snd0.at[:, :, pl.ds(0, 3)], s_s.at[0])
    wait(snd1.at[:, :, pl.ds(0, 7)], s_s.at[1])
    wait(tpiece.at[pl.ds(1, 3)], p_s.at[4])
    wait(rshard.at[:, pl.ds(0, 3)], q_s)
    wait(tdone.at[pl.ds(0, 3)], e_s)
    for p in range(2):
        for v in range(2):

            @pl.when(jnp.logical_not(same(target(0, p, v))))
            def _():
                wait(tpiece.at[0, p, v], p_s.at[2 * p + v])

    wait(fin.at[0, 0], a_r.at[0])
    wait(fin.at[pl.ds(0, 3)], a_r.at[1])

    squares = jnp.zeros((8, 512), F32)
    for i in range(16):
        block = fin[i // 4, (i // 2) % 2, i % 2]
        squares += block * block
    loads[4].wait()
    inverse = lax.rsqrt(jnp.sum(squares, axis=1, keepdims=True) * (1.0 / 8192) + 1e-05)
    for i in range(16):
        zs, us, p = i // 4, (i // 2) % 2, i % 2
        ys = pair * 2 + us if p == 0 else 3 - pair * 2 - us
        columns = pl.ds(pl.multiple_of((zs * 4 + ys) * 512, 512), 512)
        out[:, columns] = fin[zs, us, p] * inverse * gain[:, columns]

    wait(jsum.at[0, 0], a_s.at[0])
    wait(jsum.at[pl.ds(1, 3)], a_s.at[1])


def local(attn_heads, residual, low_hidden, mid_hidden, out_weight, join_weight, join_gain):
    vmem = pl.BlockSpec(memory_space=pltpu.VMEM)
    hbm = pl.BlockSpec(memory_space=pltpu.HBM)
    dma = pltpu.SemaphoreType.DMA
    rows = pl.pallas_call(
        kernel,
        out_shape=pltpu.VMEM((8, 8192), F32),
        in_specs=[hbm] * 7,
        out_specs=vmem,
        scratch_shapes=[
            pltpu.VMEM((4, 128, 512), BF16),
            pltpu.VMEM((1, 8192), F32),
            pltpu.VMEM((4, 4, 2, 2, 4, 16, 512), BF16),
            pltpu.VMEM((4, 2, 4, 16, 512), BF16),
            pltpu.VMEM((2, 4, 16, 512), BF16),
            pltpu.VMEM((4, 2, 2, 512, 512), BF16),
            pltpu.VMEM((4, 2, 4, 2, 16, 512), BF16),
            pltpu.VMEM((4, 2, 3, 2, 16, 512), BF16),
            pltpu.VMEM((4, 2, 8, 16, 512), BF16),
            pltpu.VMEM((4, 2, 7, 16, 512), BF16),
            pltpu.VMEM((4, 2, 128, 512), F32),
            pltpu.VMEM((4, 2, 4, 2, 16, 512), F32),
            pltpu.VMEM((4, 2, 2, 16, 512), BF16),
            pltpu.VMEM((4, 2, 2, 16, 512), BF16),
            pltpu.VMEM((4, 2, 16, 512), BF16),
            pltpu.VMEM((4, 2, 16, 512), BF16),
            pltpu.VMEM((4, 2, 2, 8, 512), F32),
            pltpu.VMEM((4, 2, 2, 8, 512), F32),
            dma((5,)), dma, dma((4,)),
            dma((4,)), dma, dma((4,)), dma, dma((4,)), dma, dma((4,)),
            dma, dma((4, 3, 2)), dma, dma((4, 4)),
            dma((2,)), dma((2, 4, 2)),
            dma((5,)), dma((4,)), dma, dma, dma, dma((2,)), dma((2,)), dma((2,)),
        ],
        compiler_params=pltpu.CompilerParams(
            collective_id=0, has_side_effects=True, vmem_limit_bytes=60 * 1024 * 1024
        ),
        cost_estimate=pl.CostEstimate(flops=4294967296, bytes_accessed=3145728, transcendentals=8),
    )(attn_heads, residual, low_hidden, mid_hidden, out_weight, join_weight, join_gain.reshape(1, 8192))
    return rows.astype(BF16)


def solution(mesh):
    return jax.shard_map(
        local,
        mesh=mesh,
        in_specs=(
            P("dp", "tensor"),
            P("dp", "tensor"),
            P("dp", "tensor"),
            P("dp", "tensor"),
            P("tensor", "dp"),
            P(None, "tensor", "dp"),
            P(),
        ),
        out_specs=P(("dp", "tensor"), None),
        check_vma=False,
    )
```

```python
import functools

import jax
import jax.numpy as jnp
from jax import lax
from jax.experimental import pallas as pl
from jax.experimental.pallas import tpu as pltpu
from jax.sharding import PartitionSpec as P

MESH = pl.DeviceIdType.MESH
F32 = jnp.float32
BF16 = jnp.bfloat16
ORDER = (0, 3, 1, 2)
TOP = 3


def div(a, b):
    return lax.div(a, jnp.int32(b))


def rem(a, b):
    return lax.rem(a, jnp.int32(b))


def kernel(
    attn, resid, low, mid, w_out, w_join, gain_in, out,
    inputs, gain, act, stage, rshard, w, snd0, rcv0, snd1, rcv1, acc, part, tpiece, tin, rpiece, tdone, jsum, fin,
    in_sem, x_s, x_r, wl, ws_s, ws_r, wp_s, wp_r, wf_s, wf_r,
    z_s, z_r, y_s, y_r, s_s, s_r, p_s, p_r, q_s, q_r, e_s, e_r, a_s, a_r,
):
    dp = lax.axis_index("dp")
    tensor = lax.axis_index("tensor")
    zh, y = div(dp, 4), rem(dp, 4)
    pair, u = div(y, 2), rem(y, 2)
    q, c = div(tensor, 2), rem(tensor, 2)
    x, zl = div(q, 2), rem(q, 2)
    other_u, other_c = 1 - u, 1 - c

    def dev(zh_, y_, q_, c_):
        return (zh_ * 4 + y_, q_ * 2 + c_)

    def same(device):
        return jnp.logical_and(device[0] == dp, device[1] == tensor)

    def send(src, dst, ss, rs, device):
        pltpu.make_async_remote_copy(
            src_ref=src, dst_ref=dst, send_sem=ss, recv_sem=rs, device_id=device, device_id_type=MESH
        ).start()

    def wait(ref, sem):
        pltpu.make_async_copy(ref, ref, sem).wait()

    sibling = dev(zh, y, q, other_c)
    partner = dev(zh, 3 - y, q, c)
    across = dev(zh, pair * 2 + other_u, q, c)
    z_up = dev(rem(zh + 1, 4), y, q, c)
    z_down = dev(rem(zh + 3, 4), y, q, c)

    def x_of(o):
        return rem(x + o, 4)

    def peer(ox, oz):
        return dev(zh, y, x_of(ox) * 2 + rem(zl + oz, 2), c)

    def group(j, du):
        return dev(rem(zh + j, 4), pair * 2 + rem(u + du, 2), q, c)

    def land(p):
        yd = y if p == 0 else 3 - y
        return div(yd, 2), rem(yd, 2)

    def target(j, p, v):
        return dev(rem(zh + j, 4), pair * 2 + v, x * 2 + land(p)[0], c)

    def source(fc, zs, zls):
        yd = zl * 2 + fc
        return dev(zs, yd + rem(zl + pair, 2) * (3 - 2 * yd), x * 2 + zls, c)

    loads = [
        pltpu.make_async_copy(ref, inputs.at[i], in_sem.at[i]) for i, ref in enumerate((attn, resid, low, mid))
    ]
    loads.append(pltpu.make_async_copy(gain_in, gain, in_sem.at[4]))
    for load in loads:
        load.start()

    barrier = pltpu.get_barrier_semaphore()

    def greet(device):
        pl.semaphore_signal(barrier, inc=1, device_id=device, device_id_type=MESH)

    greet(sibling)
    greet(partner)
    for o in range(1, 8):
        greet(peer(o // 2, o % 2))
    for o in range(1, 8):
        greet(group(o // 2, o % 2))
    for i in range(16):
        greet(source(i // 8, i % 8 // 2, i % 2))

    def split(slot):
        loads[slot].wait()
        rows = inputs[slot].astype(F32).reshape(8, 2, 8, 512)
        for half in range(2):
            stage[slot, half] = rows[:, half].reshape(4, 16, 512).astype(BF16)

    def weight(k):
        return w_out if k == 0 else w_join.at[k - 1]

    for k in range(4):
        pltpu.make_async_copy(weight(k), w.at[k, 0, c], wl.at[k]).start()
    for slot in range(4):
        split(slot)
    act[0, 0, u, c] = stage[0, c]
    rshard[c] = stage[1, c]
    act[1, 0, u, c] = stage[2, c]
    act[2, 0, u, c] = stage[3, c]
    pl.semaphore_wait(barrier, 32)

    def swapped(slot):
        return (act.at[0, 0, u], rshard, act.at[1, 0, u], act.at[2, 0, u])[slot]

    def swap(slot):
        send(stage.at[slot, other_c], swapped(slot).at[c], x_s, x_r.at[slot], sibling)

    def weight_near(k):
        send(weight(k), w.at[k, 0, c], ws_s, ws_r.at[k], sibling)

    def weight_far(k):
        send(weight(k), w.at[k, 1, c], wp_s, wp_r.at[k], partner)

    def weight_forward(k):
        wait(w.at[k, 1, c], wp_r.at[k])
        send(w.at[k, 1, c], w.at[k, 1, c], wf_s, wf_r.at[k], sibling)

    def weight_near_ready(k):
        wait(w.at[k, 0, c], wl.at[k])
        wait(w.at[k, 0, other_c], ws_r.at[k])

    def weight_far_ready(k):
        wait(w.at[k, 1, other_c], wf_r.at[k])

    def across_send(a, j, fc):
        piece = act.at[a, j, u, fc]
        send(piece, piece, y_s, y_r.at[a, j], across)

    def z_send(a, slot, fc, to_slot, device):
        send(act.at[a, slot, u, fc], act.at[a, to_slot, u, fc], z_s, z_r.at[a, to_slot - 1, fc], device)

    def z_wait(a, slot, fc):
        wait(act.at[a, slot, u, fc], z_r.at[a, slot - 1, fc])

    def gather_z(a):
        for i in range(2):
            z_send(a, 0, i, 3, z_up)
            z_send(a, 0, 1 - i, 1, z_down)

    def gather_y(a):
        across_send(a, 0, 0)
        across_send(a, 0, 1)

    def gather_first(a):
        z_wait(a, 3, 0)
        z_send(a, 3, 0, 2, z_up)
        across_send(a, 3, 0)
        z_wait(a, 1, 1)
        z_send(a, 1, 1, 2, z_down)
        across_send(a, 1, 1)

    def gather_second(a):
        z_wait(a, 3, 1)
        across_send(a, 3, 1)
        z_wait(a, 1, 0)
        across_send(a, 1, 0)

    def gather_last(a):
        for fc in range(2):
            z_wait(a, 2, fc)
            across_send(a, 2, fc)

    def heads_begin(half):
        z_send(0, 0, half, 3, z_up)
        z_send(0, 0, half, 1, z_down)
        across_send(0, 0, half)

    def heads_first():
        z_wait(0, 3, c)
        z_send(0, 3, c, 2, z_up)
        across_send(0, 3, c)
        z_wait(0, 1, c)
        across_send(0, 1, c)

    def heads_second():
        z_wait(0, 1, other_c)
        z_send(0, 1, other_c, 2, z_down)
        across_send(0, 1, other_c)
        z_wait(0, 3, other_c)
        across_send(0, 3, other_c)

    def gathered(a, j):
        wait(act.at[a, j, other_u], y_r.at[a, j])

    def product(a, j, p):
        total = None
        for fc in range(2):
            lhs = act[a, j, :, fc].reshape(128, 512)
            term = jnp.dot(lhs, w[a, p, fc], preferred_element_type=F32)
            total = term if total is None else total + term
        return total

    def add(own, received):
        total = own
        for o in range(received.shape[0]):
            total += received[o].astype(F32)
        return total

    def head(j, p):
        total = product(0, j, p)
        for v in range(2):
            for jb in range(4):
                start = v * 64 + jb * 16
                part[j, p, jb, v] = total[start : start + 16]
        snd0[j, p] = part[j, p].astype(BF16)
        for o in range(1, 4):
            send(snd0.at[j, p, x_of(o)], rcv0.at[j, p, o - 1], s_s.at[0], s_r.at[0, j, p], peer(o, 0))

    def joined(j, p):
        total = acc[j, p] + product(TOP, j, p)
        for owner in range(8):
            rows = jnp.concatenate([total[8 * owner : 8 * owner + 8], total[64 + 8 * owner : 72 + 8 * owner]], axis=0)
            part[j, p, owner // 2, owner % 2] = rows
            snd1[j, p, owner] = rows.astype(BF16)
        for o in range(1, 8):
            owner = x_of(o // 2) * 2 + rem(zl + o % 2, 2)
            send(snd1.at[j, p, owner], rcv1.at[j, p, o - 1], s_s.at[1], s_r.at[1, j, p], peer(o // 2, o % 2))

    def add_head(j, p):
        wait(rcv0.at[j, p], s_r.at[0, j, p])
        tpiece[j, p] = add(part[j, p, x], rcv0[j, p]).astype(BF16)
        fc = land(p)[1]
        for v in range(2):
            device = target(j, p, v)
            src, dst, rs = tpiece.at[j, p, v], tin.at[zh, fc, zl], p_r.at[zh]
            if j:
                send(src, dst, p_s.at[4], rs, device)
            else:
                me = same(device)

                @pl.when(me)
                def _():
                    pltpu.make_async_copy(src, dst, rs).start()

                @pl.when(jnp.logical_not(me))
                def _():
                    send(src, dst, p_s.at[2 * p + v], rs, device)

    def residual_out():
        for fc in range(2):
            rpiece[x, fc] = rshard[fc, x]
            for o in range(1, 4):
                send(rshard.at[fc, x_of(o)], rpiece.at[x, fc], q_s, q_r, peer(o, 0))

    def top_rows(j):
        zs = rem(zh - j + 4, 4)
        wait(tin.at[zs], p_r.at[zs])
        for fc in range(2):
            total = rpiece[zs, fc].astype(F32)
            for i in range(2):
                total += tin[zs, fc, i].astype(F32)
            tdone[zs, fc] = total.astype(BF16)

        @pl.when(zs == x)
        def _():
            for fc in range(2):
                act[TOP, 0, u, fc, x] = tdone[zs, fc]

        @pl.when(zs != x)
        def _():
            for fc in range(2):
                send(tdone.at[zs, fc], act.at[TOP, 0, u, fc, x], e_s, e_r.at[fc], dev(zh, y, zs * 2 + zl, c))

    def deliver(j):
        for p in range(2):
            wait(rcv1.at[j, p], s_r.at[1, j, p])
            total = add(part[j, p, x, zl], rcv1[j, p])
            jsum[j, 0, p] = total[:8]
            jsum[j, 1, p] = total[8:]
        for du in range(2):
            v = rem(u + du, 2)
            if j == 0 and du == 0:
                fin[zh, u] = jsum[0, u]
            else:
                send(jsum.at[j, v], fin.at[zh, u], a_s.at[min(j, 1)], a_r.at[min(j, 1)], group(j, du))

    def add_mid(j):
        gathered(2, j)
        for p in range(2):
            acc[j, p] += product(2, j, p)

    swap(0)
    heads_begin(c)
    for slot in range(1, 4):
        swap(slot)
    weight_near(0)
    for k in range(4):
        weight_far(k)
    wait(act.at[0, 0, u, other_c], x_r.at[0])
    heads_begin(other_c)
    wait(rshard.at[other_c], x_r.at[1])
    wait(act.at[1, 0, u, other_c], x_r.at[2])
    gather_y(1)
    wait(act.at[2, 0, u, other_c], x_r.at[3])
    weight_near_ready(0)
    heads_first()
    gathered(0, 0)
    head(0, 0)
    heads_second()
    gather_z(1)
    residual_out()
    weight_near(1)
    gather_last(0)
    weight_forward(0)
    gathered(0, 3)
    head(3, 0)
    weight_far_ready(0)
    head(3, 1)
    gathered(0, 1)
    head(1, 0)
    gather_first(1)
    gather_z(2)
    gathered(0, 2)
    head(2, 0)
    head(2, 1)
    head(1, 1)
    head(0, 1)
    gather_second(1)
    gather_y(2)
    weight_near(2)
    weight_near(3)
    add_head(0, 0)
    add_head(3, 0)
    add_head(3, 1)
    add_head(1, 0)
    add_head(2, 0)
    add_head(2, 1)
    add_head(1, 1)
    add_head(0, 1)
    gather_last(1)
    gather_first(2)
    gather_second(2)
    wait(rpiece.at[pl.ds(0, 3)], q_r)
    for j in ORDER:
        top_rows(j)
    for fc in range(2):
        wait(act.at[TOP, 0, u, fc, pl.ds(0, 3)], e_r.at[fc])
    gather_z(TOP)
    weight_forward(1)
    gather_y(TOP)
    weight_near_ready(1)
    for j in ORDER:
        gathered(1, j)
    weight_far_ready(1)
    for j in ORDER:
        for p in range(2):
            acc[j, p] = product(1, j, p)
    weight_forward(2)
    gather_last(2)
    gather_first(TOP)
    weight_near_ready(2)
    weight_near_ready(3)
    weight_far_ready(2)
    add_mid(0)
    gathered(TOP, 0)
    joined(0, 0)
    gather_second(TOP)
    add_mid(3)
    add_mid(1)
    gather_last(TOP)
    weight_forward(3)
    add_mid(2)
    gathered(TOP, 3)
    joined(3, 0)
    weight_far_ready(3)
    joined(3, 1)
    gathered(TOP, 1)
    joined(1, 0)
    gathered(TOP, 2)
    joined(2, 0)
    joined(2, 1)
    joined(1, 1)
    joined(0, 1)
    for j in (3, 2, 1, 0):
        deliver(j)
    wait(stage.at[:, 0], x_s)
    for sem in (ws_s, wp_s, wf_s):
        wait(w.at[:, 0, 0], sem)
    wait(act.at[:, pl.ds(0, 2)], y_s)
    wait(act.at[:, pl.ds(0, 3), 0], z_s)
    wait(snd0.at[:, :, pl.ds(0, 3)], s_s.at[0])
    wait(snd1.at[:, :, pl.ds(0, 7)], s_s.at[1])
    wait(tpiece.at[pl.ds(1, 3)], p_s.at[4])
    wait(rshard.at[:, pl.ds(0, 3)], q_s)
    wait(tdone.at[pl.ds(0, 3)], e_s)
    for p in range(2):
        for v in range(2):

            @pl.when(jnp.logical_not(same(target(0, p, v))))
            def _():
                wait(tpiece.at[0, p, v], p_s.at[2 * p + v])

    wait(fin.at[0, 0], a_r.at[0])
    wait(fin.at[pl.ds(0, 3)], a_r.at[1])

    squares = jnp.zeros((8, 512), F32)
    for i in range(16):
        block = fin[i // 4, (i // 2) % 2, i % 2]
        squares += block * block
    loads[4].wait()
    inverse = lax.rsqrt(jnp.sum(squares, axis=1, keepdims=True) * (1.0 / 8192) + 1e-05)
    for i in range(16):
        zs, us, p = i // 4, (i // 2) % 2, i % 2
        ys = pair * 2 + us if p == 0 else 3 - pair * 2 - us
        columns = pl.ds(pl.multiple_of((zs * 4 + ys) * 512, 512), 512)
        out[:, columns] = fin[zs, us, p] * inverse * gain[:, columns]

    wait(jsum.at[0, 0], a_s.at[0])
    wait(jsum.at[pl.ds(1, 3)], a_s.at[1])


def local(attn_heads, residual, low_hidden, mid_hidden, out_weight, join_weight, join_gain):
    vmem = pl.BlockSpec(memory_space=pltpu.VMEM)
    hbm = pl.BlockSpec(memory_space=pltpu.HBM)
    dma = pltpu.SemaphoreType.DMA
    rows = pl.pallas_call(
        kernel,
        out_shape=pltpu.VMEM((8, 8192), F32),
        in_specs=[hbm] * 7,
        out_specs=vmem,
        scratch_shapes=[
            pltpu.VMEM((4, 128, 512), BF16),
            pltpu.VMEM((1, 8192), F32),
            pltpu.VMEM((4, 4, 2, 2, 4, 16, 512), BF16),
            pltpu.VMEM((4, 2, 4, 16, 512), BF16),
            pltpu.VMEM((2, 4, 16, 512), BF16),
            pltpu.VMEM((4, 2, 2, 512, 512), BF16),
            pltpu.VMEM((4, 2, 4, 2, 16, 512), BF16),
            pltpu.VMEM((4, 2, 3, 2, 16, 512), BF16),
            pltpu.VMEM((4, 2, 8, 16, 512), BF16),
            pltpu.VMEM((4, 2, 7, 16, 512), BF16),
            pltpu.VMEM((4, 2, 128, 512), F32),
            pltpu.VMEM((4, 2, 4, 2, 16, 512), F32),
            pltpu.VMEM((4, 2, 2, 16, 512), BF16),
            pltpu.VMEM((4, 2, 2, 16, 512), BF16),
            pltpu.VMEM((4, 2, 16, 512), BF16),
            pltpu.VMEM((4, 2, 16, 512), BF16),
            pltpu.VMEM((4, 2, 2, 8, 512), F32),
            pltpu.VMEM((4, 2, 2, 8, 512), F32),
            dma((5,)), dma, dma((4,)),
            dma((4,)), dma, dma((4,)), dma, dma((4,)), dma, dma((4,)),
            dma, dma((4, 3, 2)), dma, dma((4, 4)),
            dma((2,)), dma((2, 4, 2)),
            dma((5,)), dma((4,)), dma, dma, dma, dma((2,)), dma((2,)), dma((2,)),
        ],
        compiler_params=pltpu.CompilerParams(
            collective_id=0, has_side_effects=True, vmem_limit_bytes=60 * 1024 * 1024
        ),
        cost_estimate=pl.CostEstimate(flops=4294967296, bytes_accessed=3145728, transcendentals=8),
    )(attn_heads, residual, low_hidden, mid_hidden, out_weight, join_weight, join_gain.reshape(1, 8192))
    return rows.astype(BF16)


def solution(mesh):
    return jax.shard_map(
        local,
        mesh=mesh,
        in_specs=(
            P("dp", "tensor"),
            P("dp", "tensor"),
            P("dp", "tensor"),
            P("dp", "tensor"),
            P("tensor", "dp"),
            P(None, "tensor", "dp"),
            P(),
        ),
        out_specs=P(("dp", "tensor"), None),
        check_vma=False,
    )
```

```python
import functools

import jax
import jax.numpy as jnp
from jax import lax
from jax.experimental import pallas as pl
from jax.experimental.pallas import tpu as pltpu
from jax.sharding import PartitionSpec as P

MESH = pl.DeviceIdType.MESH
F32 = jnp.float32
BF16 = jnp.bfloat16
ORDER = (0, 3, 1, 2)
TOP = 3


def div(a, b):
    return lax.div(a, jnp.int32(b))


def rem(a, b):
    return lax.rem(a, jnp.int32(b))


def kernel(
    attn, resid, low, mid, w_out, w_join, gain_in, out,
    inputs, gain, act, stage, rshard, w, snd0, rcv0, snd1, rcv1, acc, part, tpiece, tin, rpiece, tdone, jsum, fin,
    in_sem, x_s, x_r, wl, ws_s, ws_r, wp_s, wp_r, wf_s, wf_r,
    z_s, z_r, y_s, y_r, s_s, s_r, p_s, p_r, q_s, q_r, e_s, e_r, a_s, a_r,
):
    dp = lax.axis_index("dp")
    tensor = lax.axis_index("tensor")
    zh, y = div(dp, 4), rem(dp, 4)
    pair, u = div(y, 2), rem(y, 2)
    q, c = div(tensor, 2), rem(tensor, 2)
    x, zl = div(q, 2), rem(q, 2)
    other_u, other_c = 1 - u, 1 - c

    def dev(zh_, y_, q_, c_):
        return (zh_ * 4 + y_, q_ * 2 + c_)

    def same(device):
        return jnp.logical_and(device[0] == dp, device[1] == tensor)

    def send(src, dst, ss, rs, device):
        pltpu.make_async_remote_copy(
            src_ref=src, dst_ref=dst, send_sem=ss, recv_sem=rs, device_id=device, device_id_type=MESH
        ).start()

    def wait(ref, sem):
        pltpu.make_async_copy(ref, ref, sem).wait()

    sibling = dev(zh, y, q, other_c)
    partner = dev(zh, 3 - y, q, c)
    across = dev(zh, pair * 2 + other_u, q, c)
    z_up = dev(rem(zh + 1, 4), y, q, c)
    z_down = dev(rem(zh + 3, 4), y, q, c)

    def x_of(o):
        return rem(x + o, 4)

    def peer(ox, oz):
        return dev(zh, y, x_of(ox) * 2 + rem(zl + oz, 2), c)

    def group(j, du):
        return dev(rem(zh + j, 4), pair * 2 + rem(u + du, 2), q, c)

    def land(p):
        yd = y if p == 0 else 3 - y
        return div(yd, 2), rem(yd, 2)

    def target(j, p, v):
        return dev(rem(zh + j, 4), pair * 2 + v, x * 2 + land(p)[0], c)

    def source(fc, zs, zls):
        yd = zl * 2 + fc
        return dev(zs, yd + rem(zl + pair, 2) * (3 - 2 * yd), x * 2 + zls, c)

    loads = [
        pltpu.make_async_copy(ref, inputs.at[i], in_sem.at[i]) for i, ref in enumerate((attn, resid, low, mid))
    ]
    loads.append(pltpu.make_async_copy(gain_in, gain, in_sem.at[4]))
    for load in loads:
        load.start()

    barrier = pltpu.get_barrier_semaphore()

    def greet(device):
        pl.semaphore_signal(barrier, inc=1, device_id=device, device_id_type=MESH)

    greet(sibling)
    greet(partner)
    for o in range(1, 8):
        greet(peer(o // 2, o % 2))
    for o in range(1, 8):
        greet(group(o // 2, o % 2))
    for i in range(16):
        greet(source(i // 8, i % 8 // 2, i % 2))

    def split(slot):
        loads[slot].wait()
        rows = inputs[slot].astype(F32).reshape(8, 2, 8, 512)
        for half in range(2):
            stage[slot, half] = rows[:, half].reshape(4, 16, 512).astype(BF16)

    def weight(k):
        return w_out if k == 0 else w_join.at[k - 1]

    for k in range(4):
        pltpu.make_async_copy(weight(k), w.at[k, 0, c], wl.at[k]).start()
    for slot in range(4):
        split(slot)
    act[0, 0, u, c] = stage[0, c]
    rshard[c] = stage[1, c]
    act[1, 0, u, c] = stage[2, c]
    act[2, 0, u, c] = stage[3, c]
    pl.semaphore_wait(barrier, 32)

    def swapped(slot):
        return (act.at[0, 0, u], rshard, act.at[1, 0, u], act.at[2, 0, u])[slot]

    def swap(slot):
        send(stage.at[slot, other_c], swapped(slot).at[c], x_s, x_r.at[slot], sibling)

    def weight_near(k):
        send(weight(k), w.at[k, 0, c], ws_s, ws_r.at[k], sibling)

    def weight_far(k):
        send(weight(k), w.at[k, 1, c], wp_s, wp_r.at[k], partner)

    def weight_forward(k):
        wait(w.at[k, 1, c], wp_r.at[k])
        send(w.at[k, 1, c], w.at[k, 1, c], wf_s, wf_r.at[k], sibling)

    def weight_near_ready(k):
        wait(w.at[k, 0, c], wl.at[k])
        wait(w.at[k, 0, other_c], ws_r.at[k])

    def weight_far_ready(k):
        wait(w.at[k, 1, other_c], wf_r.at[k])

    def across_send(a, j, fc):
        piece = act.at[a, j, u, fc]
        send(piece, piece, y_s, y_r.at[a, j], across)

    def z_send(a, slot, fc, to_slot, device):
        send(act.at[a, slot, u, fc], act.at[a, to_slot, u, fc], z_s, z_r.at[a, to_slot - 1, fc], device)

    def z_wait(a, slot, fc):
        wait(act.at[a, slot, u, fc], z_r.at[a, slot - 1, fc])

    def gather_z(a):
        for i in range(2):
            z_send(a, 0, i, 3, z_up)
            z_send(a, 0, 1 - i, 1, z_down)

    def gather_y(a):
        across_send(a, 0, 0)
        across_send(a, 0, 1)

    def gather_first(a):
        z_wait(a, 3, 0)
        z_send(a, 3, 0, 2, z_up)
        across_send(a, 3, 0)
        z_wait(a, 1, 1)
        z_send(a, 1, 1, 2, z_down)
        across_send(a, 1, 1)

    def gather_second(a):
        z_wait(a, 3, 1)
        across_send(a, 3, 1)
        z_wait(a, 1, 0)
        across_send(a, 1, 0)

    def gather_last(a):
        for fc in range(2):
            z_wait(a, 2, fc)
            across_send(a, 2, fc)

    def heads_begin(half):
        z_send(0, 0, half, 3, z_up)
        z_send(0, 0, half, 1, z_down)
        across_send(0, 0, half)

    def heads_first():
        z_wait(0, 3, c)
        z_send(0, 3, c, 2, z_up)
        across_send(0, 3, c)
        z_wait(0, 1, c)
        across_send(0, 1, c)

    def heads_second():
        z_wait(0, 1, other_c)
        z_send(0, 1, other_c, 2, z_down)
        across_send(0, 1, other_c)
        z_wait(0, 3, other_c)
        across_send(0, 3, other_c)

    def gathered(a, j):
        wait(act.at[a, j, other_u], y_r.at[a, j])

    def product(a, j, p):
        total = None
        for fc in range(2):
            lhs = act[a, j, :, fc].reshape(128, 512)
            term = jnp.dot(lhs, w[a, p, fc], preferred_element_type=F32)
            total = term if total is None else total + term
        return total

    def add(own, received):
        total = own
        for o in range(received.shape[0]):
            total += received[o].astype(F32)
        return total

    def head(j, p):
        total = product(0, j, p)
        for v in range(2):
            for jb in range(4):
                start = v * 64 + jb * 16
                part[j, p, jb, v] = total[start : start + 16]
        snd0[j, p] = part[j, p].astype(BF16)
        for o in range(1, 4):
            send(snd0.at[j, p, x_of(o)], rcv0.at[j, p, o - 1], s_s.at[0], s_r.at[0, j, p], peer(o, 0))

    def joined(j, p):
        total = acc[j, p] + product(TOP, j, p)
        for owner in range(8):
            rows = jnp.concatenate([total[8 * owner : 8 * owner + 8], total[64 + 8 * owner : 72 + 8 * owner]], axis=0)
            part[j, p, owner // 2, owner % 2] = rows
            snd1[j, p, owner] = rows.astype(BF16)
        for o in range(1, 8):
            owner = x_of(o // 2) * 2 + rem(zl + o % 2, 2)
            send(snd1.at[j, p, owner], rcv1.at[j, p, o - 1], s_s.at[1], s_r.at[1, j, p], peer(o // 2, o % 2))

    def add_head(j, p):
        wait(rcv0.at[j, p], s_r.at[0, j, p])
        tpiece[j, p] = add(part[j, p, x], rcv0[j, p]).astype(BF16)
        fc = land(p)[1]
        for v in range(2):
            device = target(j, p, v)
            src, dst, rs = tpiece.at[j, p, v], tin.at[zh, fc, zl], p_r.at[zh]
            if j:
                send(src, dst, p_s.at[4], rs, device)
            else:
                me = same(device)

                @pl.when(me)
                def _():
                    pltpu.make_async_copy(src, dst, rs).start()

                @pl.when(jnp.logical_not(me))
                def _():
                    send(src, dst, p_s.at[2 * p + v], rs, device)

    def residual_out():
        for fc in range(2):
            rpiece[x, fc] = rshard[fc, x]
            for o in range(1, 4):
                send(rshard.at[fc, x_of(o)], rpiece.at[x, fc], q_s, q_r, peer(o, 0))

    def top_rows(j):
        zs = rem(zh - j + 4, 4)
        wait(tin.at[zs], p_r.at[zs])
        for fc in range(2):
            total = rpiece[zs, fc].astype(F32)
            for i in range(2):
                total += tin[zs, fc, i].astype(F32)
            tdone[zs, fc] = total.astype(BF16)

        @pl.when(zs == x)
        def _():
            for fc in range(2):
                act[TOP, 0, u, fc, x] = tdone[zs, fc]

        @pl.when(zs != x)
        def _():
            for fc in range(2):
                send(tdone.at[zs, fc], act.at[TOP, 0, u, fc, x], e_s, e_r.at[fc], dev(zh, y, zs * 2 + zl, c))

    def deliver(j):
        for p in range(2):
            wait(rcv1.at[j, p], s_r.at[1, j, p])
            total = add(part[j, p, x, zl], rcv1[j, p])
            jsum[j, 0, p] = total[:8]
            jsum[j, 1, p] = total[8:]
        for du in range(2):
            v = rem(u + du, 2)
            if j == 0 and du == 0:
                fin[zh, u] = jsum[0, u]
            else:
                send(jsum.at[j, v], fin.at[zh, u], a_s.at[min(j, 1)], a_r.at[min(j, 1)], group(j, du))

    def add_mid(j):
        gathered(2, j)
        for p in range(2):
            acc[j, p] += product(2, j, p)

    swap(0)
    heads_begin(c)
    for slot in range(1, 4):
        swap(slot)
    weight_near(0)
    for k in range(4):
        weight_far(k)
    wait(act.at[0, 0, u, other_c], x_r.at[0])
    heads_begin(other_c)
    wait(rshard.at[other_c], x_r.at[1])
    wait(act.at[1, 0, u, other_c], x_r.at[2])
    gather_y(1)
    wait(act.at[2, 0, u, other_c], x_r.at[3])
    weight_near_ready(0)
    heads_first()
    gathered(0, 0)
    head(0, 0)
    heads_second()
    gather_z(1)
    residual_out()
    weight_near(1)
    gather_last(0)
    weight_forward(0)
    gathered(0, 3)
    head(3, 0)
    weight_far_ready(0)
    head(3, 1)
    gathered(0, 1)
    head(1, 0)
    gather_first(1)
    gather_z(2)
    gathered(0, 2)
    head(2, 0)
    head(2, 1)
    head(1, 1)
    head(0, 1)
    gather_second(1)
    gather_y(2)
    weight_near(2)
    weight_near(3)
    add_head(0, 0)
    add_head(3, 0)
    add_head(3, 1)
    add_head(1, 0)
    add_head(2, 0)
    add_head(2, 1)
    add_head(1, 1)
    add_head(0, 1)
    gather_last(1)
    gather_first(2)
    gather_second(2)
    wait(rpiece.at[pl.ds(0, 3)], q_r)
    for j in ORDER:
        top_rows(j)
    for fc in range(2):
        wait(act.at[TOP, 0, u, fc, pl.ds(0, 3)], e_r.at[fc])
    gather_z(TOP)
    weight_forward(1)
    gather_y(TOP)
    weight_near_ready(1)
    for j in ORDER:
        gathered(1, j)
    weight_far_ready(1)
    for j in ORDER:
        for p in range(2):
            acc[j, p] = product(1, j, p)
    weight_forward(2)
    gather_last(2)
    gather_first(TOP)
    weight_near_ready(2)
    weight_near_ready(3)
    weight_far_ready(2)
    add_mid(0)
    gathered(TOP, 0)
    joined(0, 0)
    gather_second(TOP)
    add_mid(3)
    add_mid(1)
    gather_last(TOP)
    weight_forward(3)
    add_mid(2)
    gathered(TOP, 3)
    joined(3, 0)
    weight_far_ready(3)
    joined(3, 1)
    gathered(TOP, 1)
    joined(1, 0)
    joined(1, 1)
    gathered(TOP, 2)
    joined(2, 0)
    joined(2, 1)
    joined(0, 1)
    for j in (3, 1, 2, 0):
        deliver(j)
    wait(stage.at[:, 0], x_s)
    for sem in (ws_s, wp_s, wf_s):
        wait(w.at[:, 0, 0], sem)
    wait(act.at[:, pl.ds(0, 2)], y_s)
    wait(act.at[:, pl.ds(0, 3), 0], z_s)
    wait(snd0.at[:, :, pl.ds(0, 3)], s_s.at[0])
    wait(snd1.at[:, :, pl.ds(0, 7)], s_s.at[1])
    wait(tpiece.at[pl.ds(1, 3)], p_s.at[4])
    wait(rshard.at[:, pl.ds(0, 3)], q_s)
    wait(tdone.at[pl.ds(0, 3)], e_s)
    for p in range(2):
        for v in range(2):

            @pl.when(jnp.logical_not(same(target(0, p, v))))
            def _():
                wait(tpiece.at[0, p, v], p_s.at[2 * p + v])

    wait(fin.at[0, 0], a_r.at[0])
    wait(fin.at[pl.ds(0, 3)], a_r.at[1])

    squares = jnp.zeros((8, 512), F32)
    for i in range(16):
        block = fin[i // 4, (i // 2) % 2, i % 2]
        squares += block * block
    loads[4].wait()
    inverse = lax.rsqrt(jnp.sum(squares, axis=1, keepdims=True) * (1.0 / 8192) + 1e-05)
    for i in range(16):
        zs, us, p = i // 4, (i // 2) % 2, i % 2
        ys = pair * 2 + us if p == 0 else 3 - pair * 2 - us
        columns = pl.ds(pl.multiple_of((zs * 4 + ys) * 512, 512), 512)
        out[:, columns] = fin[zs, us, p] * inverse * gain[:, columns]

    wait(jsum.at[0, 0], a_s.at[0])
    wait(jsum.at[pl.ds(1, 3)], a_s.at[1])


def local(attn_heads, residual, low_hidden, mid_hidden, out_weight, join_weight, join_gain):
    vmem = pl.BlockSpec(memory_space=pltpu.VMEM)
    hbm = pl.BlockSpec(memory_space=pltpu.HBM)
    dma = pltpu.SemaphoreType.DMA
    rows = pl.pallas_call(
        kernel,
        out_shape=pltpu.VMEM((8, 8192), F32),
        in_specs=[hbm] * 7,
        out_specs=vmem,
        scratch_shapes=[
            pltpu.VMEM((4, 128, 512), BF16),
            pltpu.VMEM((1, 8192), F32),
            pltpu.VMEM((4, 4, 2, 2, 4, 16, 512), BF16),
            pltpu.VMEM((4, 2, 4, 16, 512), BF16),
            pltpu.VMEM((2, 4, 16, 512), BF16),
            pltpu.VMEM((4, 2, 2, 512, 512), BF16),
            pltpu.VMEM((4, 2, 4, 2, 16, 512), BF16),
            pltpu.VMEM((4, 2, 3, 2, 16, 512), BF16),
            pltpu.VMEM((4, 2, 8, 16, 512), BF16),
            pltpu.VMEM((4, 2, 7, 16, 512), BF16),
            pltpu.VMEM((4, 2, 128, 512), F32),
            pltpu.VMEM((4, 2, 4, 2, 16, 512), F32),
            pltpu.VMEM((4, 2, 2, 16, 512), BF16),
            pltpu.VMEM((4, 2, 2, 16, 512), BF16),
            pltpu.VMEM((4, 2, 16, 512), BF16),
            pltpu.VMEM((4, 2, 16, 512), BF16),
            pltpu.VMEM((4, 2, 2, 8, 512), F32),
            pltpu.VMEM((4, 2, 2, 8, 512), F32),
            dma((5,)), dma, dma((4,)),
            dma((4,)), dma, dma((4,)), dma, dma((4,)), dma, dma((4,)),
            dma, dma((4, 3, 2)), dma, dma((4, 4)),
            dma((2,)), dma((2, 4, 2)),
            dma((5,)), dma((4,)), dma, dma, dma, dma((2,)), dma((2,)), dma((2,)),
        ],
        compiler_params=pltpu.CompilerParams(
            collective_id=0, has_side_effects=True, vmem_limit_bytes=60 * 1024 * 1024
        ),
        cost_estimate=pl.CostEstimate(flops=4294967296, bytes_accessed=3145728, transcendentals=8),
    )(attn_heads, residual, low_hidden, mid_hidden, out_weight, join_weight, join_gain.reshape(1, 8192))
    return rows.astype(BF16)


def solution(mesh):
    return jax.shard_map(
        local,
        mesh=mesh,
        in_specs=(
            P("dp", "tensor"),
            P("dp", "tensor"),
            P("dp", "tensor"),
            P("dp", "tensor"),
            P("tensor", "dp"),
            P(None, "tensor", "dp"),
            P(),
        ),
        out_specs=P(("dp", "tensor"), None),
        check_vma=False,
    )
```
